32 devices in a mesh: shot: 8 (over y, x, core), rcv: 4 (over z).
Axes of the slice: x: 2, y: 2, z: 4, core: 2. Of those that a mesh axis runs over, the one named last changes fastest.
Arguments:
- data: bfloat16 [48, 1024, 256], P('shot', 'rcv'), may hold values from -6 to 6
- surface_traces: bfloat16 [128, 1024, 256], P('shot', 'rcv'), may hold values from -6 to 6
- primaries: bfloat16 [48, 64, 64], P('shot', 'rcv'), may hold values from -0.09375 to 0.09375
- panel_owner: int32 [4], replicated, may hold values from 0 to 7, as said below
Outputs:
- residual: bfloat16 [48, 1024, 256], P('shot', 'rcv')
The draws below stay inside these ranges and needn't reach their ends.
Inputs may be any that keep to these rules, and one draw needn't show every extreme that they name: panel_owner holds 4 distinct indices of the shot axis, in an order drawn from the seed.
All inputs are finite; a program needn't handle non-finite values.
Results may differ from the reference program's by a relative error of at most 0.001.
Values may be sent and summed in bfloat16 or wider, within the bound.
No kernel may reach another device: no remote copies, remote signals or barrier semaphores. Data moves between devices by JAX's collectives and lax.ppermute only.
A program may use at most 128 MiB of HBM per device.

```python
import jax
import jax.numpy as jnp
from jax import lax

R = 1024
T_SIZE = 256
TAPS = 64
KP = 16
PANELS = 4
K = 64
SHOTS = 48
SLOTS = 128
N_SHOT = 8


def draw_panel_owner(key, part):
    first_key = jax.random.fold_in(key, 11)
    second_key = jax.random.fold_in(key, 23)
    middle = jax.random.permutation(first_key, N_SHOT - 2)[:PANELS - 2] + 1
    chosen = jnp.concatenate([jnp.array([0, N_SHOT - 1], jnp.int32), middle.astype(jnp.int32)])
    return jax.random.permutation(second_key, chosen).astype(jnp.int32)


def block_scale(key, dims, cuts, low, high):
    gain = 1.0
    for dim, shards_of in cuts:
        steps = jax.random.uniform(jax.random.fold_in(jax.random.fold_in(key, 6), dim), (shards_of,), jnp.float32, low / len(cuts), high / len(cuts))
        gain = gain * jnp.repeat(jnp.exp(steps), dims[dim] // shards_of).reshape((-1,) + (1,) * (len(dims) - 1 - dim))
    return gain


def centred(stream_key, extent, spread, limit, pieces=(), held_as=jnp.bfloat16):
    values = jax.random.normal(stream_key, extent, jnp.float32) * spread
    if len(pieces) > 0:
        values = block_scale(stream_key, extent, pieces, -0.22, 0.18) * values
    return jnp.clip(values, min=-limit, max=limit).astype(held_as)


def setup_inputs(seed: int = 0) -> dict:
    splits = jax.random.split(jax.random.key(seed), 5)
    data = centred(splits[0], (SHOTS, R, T_SIZE), 1.0, 6.0, ((0, 8), (1, 4)))
    surface_traces = centred(splits[1], (SLOTS, R, T_SIZE), 1.0, 6.0, ((0, 8), (1, 4)))
    primaries = centred(splits[2], (SHOTS, K, TAPS), (K * TAPS) ** -0.5, 0.09375, ((0, 8), (1, 4)))
    panel_owner = draw_panel_owner(jax.random.fold_in(splits[4], 71), 0)
    return dict(data=data, surface_traces=surface_traces, primaries=primaries, panel_owner=panel_owner)


def reference(data, surface_traces, primaries, panel_owner):
    owner_slots = surface_traces.reshape(N_SHOT, KP, R, T_SIZE)
    window = jnp.take(owner_slots, panel_owner.astype(jnp.int32), axis=0).reshape(K, R, T_SIZE)
    length = 2 * T_SIZE
    window_freq = jnp.fft.rfft(window.astype(jnp.float32), n=length, axis=-1)
    prim_freq = jnp.fft.rfft(primaries.astype(jnp.float32), n=length, axis=-1)

    def one_shot(spectra):
        mult_freq = jnp.einsum('kf,krf->rf', spectra, window_freq)
        return jnp.fft.irfft(mult_freq, n=length, axis=-1)[:, :T_SIZE]

    multiples = lax.map(one_shot, prim_freq)
    return (data.astype(jnp.float32) - multiples).astype(jnp.bfloat16)
```

```python
import functools

import jax
import jax.numpy as jnp
from jax import lax
from jax.experimental import pallas as pl
from jax.experimental.pallas import tpu as pltpu
from jax.sharding import PartitionSpec as P

CORE, ACROSS, DOWN = 1, 2, 4
SQUARE = 8
CHUNKS = 2
VMEM_BYTES = 56 * 1024 * 1024


def broadcast(value, axis, root):
    mine = lax.axis_index(axis) == root
    return lax.psum(jnp.where(mine, value, jnp.zeros_like(value)), axis)


def shift_table(taps, block):
    shape = (2, taps, block, block)
    lag_index, tap_index, in_index, out_index = (lax.broadcasted_iota(jnp.int32, shape, dim) for dim in range(4))
    distance = out_index - in_index + lag_index * block
    return (distance == tap_index).astype(jnp.bfloat16)


def band_matrices(panel_prim, shift_ones):
    bands = jnp.einsum("skt,ltio->lskio", panel_prim, shift_ones, preferred_element_type=jnp.float32)
    return bands.astype(jnp.bfloat16)


def convolve(traces, bands, block):
    point_count, row_count, length = traces.shape
    blocks = traces.reshape(point_count, row_count, length // block, block)
    earlier = jnp.concatenate([jnp.zeros_like(blocks[:, :, :1]), blocks[:, :, :-1]], axis=2)
    stacked = jnp.stack([blocks, earlier])
    product = jnp.einsum("lkrbi,lskio->srbo", stacked, bands, preferred_element_type=jnp.float32)
    return product.reshape(bands.shape[1], row_count, length)


def summed_broadcasts(data, surface_traces, primaries, panel_owner):
    points, taps = surface_traces.shape[0], primaries.shape[2]
    shift_ones = shift_table(taps, 2 * taps)
    summed = jnp.zeros(data.shape, jnp.float32)
    panels_here = primaries.shape[1] // points
    for panel_id in range(panel_owner.shape[0]):
        first_point = panel_id % panels_here * points
        panel_prim = broadcast(primaries, "rcv", panel_id // panels_here)[:, first_point : first_point + points]
        traces = broadcast(surface_traces, "shot", panel_owner[panel_id])
        summed = summed + convolve(traces, band_matrices(panel_prim, shift_ones), 2 * taps)
    return (data.astype(jnp.float32) - summed).astype(jnp.bfloat16)


def flip(value, bit):
    return lax.ppermute(value, "shot", [(i, i ^ bit) for i in range(SQUARE)])


def band_kernel(place_ref, taps_ref, band_ref):
    shots, points, width = taps_ref.shape[1:]
    rows = width // 2

    def point(k, carry):
        for s in range(shots):
            row = taps_ref[0, s, pl.ds(k, 1), :]
            spread = pltpu.roll(jnp.broadcast_to(row, (rows, width)), 0, 1, stride=1, stride_axis=0)
            band_ref[pl.ds(pl.multiple_of(k * rows, rows), rows), s * width : (s + 1) * width] = spread.astype(jnp.bfloat16)
        return carry

    lax.fori_loop(0, points, point, 0)


def bands_of(blocks, place):
    panels, shots, points, width = blocks.shape
    height = points * width // 2
    return pl.pallas_call(
        band_kernel,
        out_shape=jax.ShapeDtypeStruct((panels * height, shots * width), jnp.bfloat16),
        grid_spec=pltpu.PrefetchScalarGridSpec(
            num_scalar_prefetch=1,
            grid=(panels,),
            in_specs=[pl.BlockSpec((1, shots, points, width), lambda p, place: (lax.rem(place[2] - p + panels, panels), 0, 0, 0))],
            out_specs=pl.BlockSpec((height, shots * width), lambda p, place: (p, 0)),
        ),
        compiler_params=pltpu.CompilerParams(vmem_limit_bytes=VMEM_BYTES),
        cost_estimate=pl.CostEstimate(flops=panels * height * shots * width * 8, bytes_accessed=panels * height * shots * width * 2, transcendentals=0),
        name="bands",
    )(place, blocks)


def source_of(panel, owner_ref, chip):
    panels = owner_ref.shape[0]

    def held(place):
        count = jnp.int32(0)
        for other in range(panels):
            count = count + (owner_ref[other] // 2 == place).astype(jnp.int32)
        return count

    owner = owner_ref[panel]
    there, second = owner // 2, lax.rem(owner, 2) == 1
    both = held(there) == 2
    across_full, down_full = held(chip ^ 1) == 2, held(chip ^ 2) == 2
    own = jnp.where(both & second, 1, 0)
    across = jnp.where(both & second, 4, 2)
    down = jnp.where(both & jnp.logical_not(second), 5, 3)
    single = jnp.where(down_full, 4, 5)
    double = jnp.where(second, jnp.where(across_full, 7, 4), jnp.where(down_full, 6, 5))
    diagonal = jnp.where(both, double, single)
    return jnp.where(there == chip, own, jnp.where(there == (chip ^ 1), across, jnp.where(there == (chip ^ 2), down, diagonal)))


def residual_kernel(owner_ref, place_ref, *refs):
    count = len(refs) - 10
    sources = refs[:count]
    band_ref, mine_ref, other_ref, out_mine_ref, out_other_ref, window, spread, total, arrived, _ = refs[count:]
    panel = pl.program_id(0)
    panels = pl.num_programs(0)
    points, rows, length = window.shape[1:]
    width = 128
    half = width // 2
    blocks = length // half

    @pl.when(panel == 0)
    def _():
        for p in range(window.shape[0]):
            chosen = source_of(p, owner_ref, place_ref[0])
            for index, source in enumerate(sources):
                @pl.when(chosen == index)
                def _():
                    pltpu.make_async_copy(source, window.at[p], arrived.at[p]).start()

    pltpu.make_async_copy(sources[0], window.at[panel], arrived.at[panel]).wait()
    low = lax.broadcasted_iota(jnp.int32, (rows, width), 1) < half
    for j in range(points // 2):
        for c in range(length // width):
            first = window[panel, 2 * j, :, c * width : (c + 1) * width].astype(jnp.float32)
            second = window[panel, 2 * j + 1, :, c * width : (c + 1) * width].astype(jnp.float32)
            even = jnp.where(low, first, pltpu.roll(second, half, 1))
            odd = jnp.where(low, pltpu.roll(first, half, 1), second)
            spread[2 * c * rows : (2 * c + 1) * rows, j * width : (j + 1) * width] = even.astype(jnp.bfloat16)
            spread[(2 * c + 1) * rows : (2 * c + 2) * rows, j * width : (j + 1) * width] = odd.astype(jnp.bfloat16)
    product = jnp.dot(spread[...], band_ref[...], preferred_element_type=jnp.float32)

    @pl.when(panel == 0)
    def _():
        total[...] = product

    @pl.when(panel > 0)
    def _():
        total[...] += product

    @pl.when(panel == panels - 1)
    def _():
        shots = mine_ref.shape[0]
        for s in range(2 * shots):
            data_ref, out_ref = (mine_ref, out_mine_ref) if s < shots else (other_ref, out_other_ref)

            def part(b):
                return total[b * rows : (b + 1) * rows, s * width : (s + 1) * width]

            for c in range(length // width):
                before = part(2 * c - 1) if c > 0 else jnp.zeros((rows, width), jnp.float32)
                moved = pltpu.roll(jnp.where(low, part(2 * c + 1), before), half, 1)
                here = data_ref[s % shots, :, c * width : (c + 1) * width].astype(jnp.float32)
                out_ref[s % shots, :, c * width : (c + 1) * width] = (here - (part(2 * c) + moved)).astype(jnp.bfloat16)


def residual_of(chunk, owner, place, sources, bands, data, other_data):
    points, rows, length = sources[0].shape
    panels = owner.shape[0]
    shots = data.shape[0]
    height, columns = bands.shape[0] // panels, bands.shape[1]
    piece = jax.ShapeDtypeStruct((shots, rows, length), jnp.bfloat16)
    return pl.pallas_call(
        residual_kernel,
        out_shape=(piece, piece),
        grid_spec=pltpu.PrefetchScalarGridSpec(
            num_scalar_prefetch=2,
            grid=(panels,),
            in_specs=[pl.BlockSpec(memory_space=pl.ANY)] * len(sources)
            + [
                pl.BlockSpec((height, columns), lambda p, owner, place: (p, 0)),
                pl.BlockSpec((shots, rows, length), lambda p, owner, place: (0, place[1] * CHUNKS + chunk, 0)),
                pl.BlockSpec((shots, rows, length), lambda p, owner, place: (0, chunk, 0)),
            ],
            out_specs=[pl.BlockSpec((shots, rows, length), lambda p, owner, place: (0, 0, 0))] * 2,
            scratch_shapes=[
                pltpu.VMEM((panels, points, rows, length), jnp.bfloat16),
                pltpu.VMEM((rows * length // 64, height), jnp.bfloat16),
                pltpu.VMEM((rows * length // 64, columns), jnp.float32),
                pltpu.SemaphoreType.DMA((panels,)),
                pltpu.SemaphoreType.DMA,
            ],
        ),
        compiler_params=pltpu.CompilerParams(vmem_limit_bytes=VMEM_BYTES),
        cost_estimate=pl.CostEstimate(flops=2 * rows * length // 64 * bands.size, bytes_accessed=2 * bands.size, transcendentals=0),
        name="residual",
    )(owner, place, *sources, bands, data, other_data)


def square_shards(data, surface_traces, primaries, panel_owner):
    panels = panel_owner.shape[0]
    receivers = data.shape[1]
    side = receivers // 2
    rows = side // CHUNKS
    taps = primaries.shape[2]
    me = lax.axis_index("shot")
    core, chip = me % 2, me // 2
    first_owns = jnp.any(panel_owner == 2 * chip)
    second_owns = jnp.any(panel_owner == 2 * chip + 1)
    mine_is_a = first_owns == (core == 0)
    mine_is_b = second_owns == (core == 1)
    both = first_owns & second_owns
    holds_two = [jnp.sum(panel_owner // 2 == place) == 2 for place in range(SQUARE // 2)]
    neighbours_full = functools.reduce(
        jnp.logical_or, [holds_two[place] & holds_two[place ^ bit] for place in range(SQUARE // 2) for bit in (1, 2) if place < place ^ bit]
    )
    place = jnp.stack([chip, core, lax.axis_index("rcv")]).astype(jnp.int32)

    def run(third):
        own_a, own_b = [], []
        for chunk in range(CHUNKS):
            here = lax.dynamic_slice_in_dim(surface_traces, core * side + chunk * rows, rows, axis=1)
            there = lax.dynamic_slice_in_dim(surface_traces, (1 - core) * side + chunk * rows, rows, axis=1)
            met = flip(there, CORE)
            own_a.append(jnp.where(mine_is_a, here, met))
            own_b.append(jnp.where(mine_is_b, here, met))
        across = [flip(a, ACROSS) for a in own_a]
        down = [flip(b, DOWN) for b in own_b]

        ring = lax.axis_size("rcv")
        blocks = [primaries] + [lax.ppermute(primaries, "rcv", [(i, (i + j) % ring) for i in range(ring)]) for j in range(1, ring)]
        blocks = jnp.stack(blocks)
        blocks = jnp.concatenate([blocks, flip(blocks, CORE)], axis=1)
        blocks = jnp.pad(blocks.astype(jnp.float32), ((0, 0), (0, 0), (0, 0), (0, taps)))
        bands = bands_of(blocks, place)
        other_data = flip(lax.dynamic_slice_in_dim(data, (1 - core) * side, side, axis=1), CORE)

        kept, returned = [], []
        for chunk in range(CHUNKS):
            across_again = flip(jnp.where(both, own_b[chunk], down[chunk]), ACROSS)
            down_again = flip(jnp.where(both, own_a[chunk], across[chunk]), DOWN)
            sources = [own_a[chunk], own_b[chunk], across[chunk], down[chunk], across_again, down_again]
            if third:
                sources += [flip(down_again, ACROSS), flip(across_again, DOWN)]
            mine, others = residual_of(chunk, panel_owner, place, sources, bands, data, other_data)
            kept.append(mine)
            returned.append(flip(others, CORE))
        return jnp.where(core == 0, jnp.concatenate(kept + returned, axis=1), jnp.concatenate(returned + kept, axis=1))

    return lax.cond(neighbours_full, functools.partial(run, True), functools.partial(run, False))


def solution(mesh):
    placed = (P("shot", "rcv", None), P("shot", "rcv", None), P("shot", "rcv", None), P())
    shards = square_shards if mesh.shape["shot"] == SQUARE else summed_broadcasts
    return jax.shard_map(shards, mesh=mesh, in_specs=placed, out_specs=P("shot", "rcv", None), check_vma=False)
```

```python
import functools

import jax
import jax.numpy as jnp
from jax import lax
from jax.experimental import pallas as pl
from jax.experimental.pallas import tpu as pltpu
from jax.sharding import PartitionSpec as P

CORE, ACROSS, DOWN = 1, 2, 4
SQUARE = 8
CHUNKS = 2
VMEM_BYTES = 20 * 1024 * 1024


def broadcast(value, axis, root):
    mine = lax.axis_index(axis) == root
    return lax.psum(jnp.where(mine, value, jnp.zeros_like(value)), axis)


def shift_table(taps, block):
    shape = (2, taps, block, block)
    lag_index, tap_index, in_index, out_index = (lax.broadcasted_iota(jnp.int32, shape, dim) for dim in range(4))
    distance = out_index - in_index + lag_index * block
    return (distance == tap_index).astype(jnp.bfloat16)


def band_matrices(panel_prim, shift_ones):
    bands = jnp.einsum("skt,ltio->lskio", panel_prim, shift_ones, preferred_element_type=jnp.float32)
    return bands.astype(jnp.bfloat16)


def convolve(traces, bands, block):
    point_count, row_count, length = traces.shape
    blocks = traces.reshape(point_count, row_count, length // block, block)
    earlier = jnp.concatenate([jnp.zeros_like(blocks[:, :, :1]), blocks[:, :, :-1]], axis=2)
    stacked = jnp.stack([blocks, earlier])
    product = jnp.einsum("lkrbi,lskio->srbo", stacked, bands, preferred_element_type=jnp.float32)
    return product.reshape(bands.shape[1], row_count, length)


def summed_broadcasts(data, surface_traces, primaries, panel_owner):
    points, taps = surface_traces.shape[0], primaries.shape[2]
    shift_ones = shift_table(taps, 2 * taps)
    summed = jnp.zeros(data.shape, jnp.float32)
    panels_here = primaries.shape[1] // points
    for panel_id in range(panel_owner.shape[0]):
        first_point = panel_id % panels_here * points
        panel_prim = broadcast(primaries, "rcv", panel_id // panels_here)[:, first_point : first_point + points]
        traces = broadcast(surface_traces, "shot", panel_owner[panel_id])
        summed = summed + convolve(traces, band_matrices(panel_prim, shift_ones), 2 * taps)
    return (data.astype(jnp.float32) - summed).astype(jnp.bfloat16)


def flip(value, bit):
    return lax.ppermute(value, "shot", [(i, i ^ bit) for i in range(SQUARE)])


def band_kernel(place_ref, taps_ref, band_ref):
    shots, points, width = taps_ref.shape[1:]
    rows = width // 2

    def point(k, carry):
        for s in range(shots):
            row = taps_ref[0, s, pl.ds(k, 1), :]
            spread = pltpu.roll(jnp.broadcast_to(row, (rows, width)), 0, 1, stride=1, stride_axis=0)
            band_ref[pl.ds(pl.multiple_of(k * rows, rows), rows), s * width : (s + 1) * width] = spread.astype(jnp.bfloat16)
        return carry

    lax.fori_loop(0, points, point, 0)


def bands_of(blocks, place):
    panels, shots, points, width = blocks.shape
    height = points * width // 2
    return pl.pallas_call(
        band_kernel,
        out_shape=jax.ShapeDtypeStruct((panels * height, shots * width), jnp.bfloat16),
        grid_spec=pltpu.PrefetchScalarGridSpec(
            num_scalar_prefetch=1,
            grid=(panels,),
            in_specs=[pl.BlockSpec((1, shots, points, width), lambda p, place: (lax.rem(place[2] - p + panels, panels), 0, 0, 0))],
            out_specs=pl.BlockSpec((height, shots * width), lambda p, place: (p, 0)),
        ),
        compiler_params=pltpu.CompilerParams(vmem_limit_bytes=VMEM_BYTES),
        cost_estimate=pl.CostEstimate(flops=panels * height * shots * width * 8, bytes_accessed=panels * height * shots * width * 2, transcendentals=0),
        name="bands",
    )(place, blocks)


def source_of(panel, owner_ref, chip):
    panels = owner_ref.shape[0]

    def held(place):
        count = jnp.int32(0)
        for other in range(panels):
            count = count + (owner_ref[other] // 2 == place).astype(jnp.int32)
        return count

    owner = owner_ref[panel]
    there, second = owner // 2, lax.rem(owner, 2) == 1
    both = held(there) == 2
    across_full, down_full = held(chip ^ 1) == 2, held(chip ^ 2) == 2
    own = jnp.where(both & second, 1, 0)
    across = jnp.where(both & second, 4, 2)
    down = jnp.where(both & jnp.logical_not(second), 5, 3)
    single = jnp.where(down_full, 4, 5)
    double = jnp.where(second, jnp.where(across_full, 7, 4), jnp.where(down_full, 6, 5))
    diagonal = jnp.where(both, double, single)
    return jnp.where(there == chip, own, jnp.where(there == (chip ^ 1), across, jnp.where(there == (chip ^ 2), down, diagonal)))


def residual_kernel(owner_ref, place_ref, *refs):
    count = len(refs) - 10
    sources = refs[:count]
    band_ref, mine_ref, other_ref, out_mine_ref, out_other_ref, window, spread, total, arrived, _ = refs[count:]
    panel = pl.program_id(0)
    panels = pl.num_programs(0)
    points, rows, length = window.shape[1:]
    width = 128
    half = width // 2
    blocks = length // half

    @pl.when(panel == 0)
    def _():
        for p in range(window.shape[0]):
            chosen = source_of(p, owner_ref, place_ref[0])
            for index, source in enumerate(sources):
                @pl.when(chosen == index)
                def _():
                    pltpu.make_async_copy(source, window.at[p], arrived.at[p]).start()

    pltpu.make_async_copy(sources[0], window.at[panel], arrived.at[panel]).wait()
    low = lax.broadcasted_iota(jnp.int32, (rows, width), 1) < half
    for j in range(points // 2):
        for c in range(length // width):
            first = window[panel, 2 * j, :, c * width : (c + 1) * width].astype(jnp.float32)
            second = window[panel, 2 * j + 1, :, c * width : (c + 1) * width].astype(jnp.float32)
            even = jnp.where(low, first, pltpu.roll(second, half, 1))
            odd = jnp.where(low, pltpu.roll(first, half, 1), second)
            spread[2 * c * rows : (2 * c + 1) * rows, j * width : (j + 1) * width] = even.astype(jnp.bfloat16)
            spread[(2 * c + 1) * rows : (2 * c + 2) * rows, j * width : (j + 1) * width] = odd.astype(jnp.bfloat16)
    product = jnp.dot(spread[...], band_ref[...], preferred_element_type=jnp.float32)

    @pl.when(panel == 0)
    def _():
        total[...] = product

    @pl.when(panel > 0)
    def _():
        total[...] += product

    @pl.when(panel == panels - 1)
    def _():
        shots = mine_ref.shape[0]
        for s in range(2 * shots):
            data_ref, out_ref = (mine_ref, out_mine_ref) if s < shots else (other_ref, out_other_ref)

            def part(b):
                return total[b * rows : (b + 1) * rows, s * width : (s + 1) * width]

            for c in range(length // width):
                before = part(2 * c - 1) if c > 0 else jnp.zeros((rows, width), jnp.float32)
                moved = pltpu.roll(jnp.where(low, part(2 * c + 1), before), half, 1)
                here = data_ref[s % shots, :, c * width : (c + 1) * width].astype(jnp.float32)
                out_ref[s % shots, :, c * width : (c + 1) * width] = (here - (part(2 * c) + moved)).astype(jnp.bfloat16)


def residual_of(chunk, owner, place, sources, bands, data, other_data):
    points, rows, length = sources[0].shape
    panels = owner.shape[0]
    shots = data.shape[0]
    height, columns = bands.shape[0] // panels, bands.shape[1]
    piece = jax.ShapeDtypeStruct((shots, rows, length), jnp.bfloat16)
    return pl.pallas_call(
        residual_kernel,
        out_shape=(piece, piece),
        grid_spec=pltpu.PrefetchScalarGridSpec(
            num_scalar_prefetch=2,
            grid=(panels,),
            in_specs=[pl.BlockSpec(memory_space=pl.ANY)] * len(sources)
            + [
                pl.BlockSpec((height, columns), lambda p, owner, place: (p, 0)),
                pl.BlockSpec((shots, rows, length), lambda p, owner, place: (0, place[1] * CHUNKS + chunk, 0)),
                pl.BlockSpec((shots, rows, length), lambda p, owner, place: (0, chunk, 0)),
            ],
            out_specs=[pl.BlockSpec((shots, rows, length), lambda p, owner, place: (0, 0, 0))] * 2,
            scratch_shapes=[
                pltpu.VMEM((panels, points, rows, length), jnp.bfloat16),
                pltpu.VMEM((rows * length // 64, height), jnp.bfloat16),
                pltpu.VMEM((rows * length // 64, columns), jnp.float32),
                pltpu.SemaphoreType.DMA((panels,)),
                pltpu.SemaphoreType.DMA,
            ],
        ),
        compiler_params=pltpu.CompilerParams(vmem_limit_bytes=VMEM_BYTES),
        cost_estimate=pl.CostEstimate(flops=2 * rows * length // 64 * bands.size, bytes_accessed=2 * bands.size, transcendentals=0),
        name="residual",
    )(owner, place, *sources, bands, data, other_data)


def square_shards(data, surface_traces, primaries, panel_owner):
    panels = panel_owner.shape[0]
    receivers = data.shape[1]
    side = receivers // 2
    rows = side // CHUNKS
    taps = primaries.shape[2]
    me = lax.axis_index("shot")
    core, chip = me % 2, me // 2
    first_owns = jnp.any(panel_owner == 2 * chip)
    second_owns = jnp.any(panel_owner == 2 * chip + 1)
    mine_is_a = first_owns == (core == 0)
    mine_is_b = second_owns == (core == 1)
    both = first_owns & second_owns
    holds_two = [jnp.sum(panel_owner // 2 == place) == 2 for place in range(SQUARE // 2)]
    neighbours_full = functools.reduce(
        jnp.logical_or, [holds_two[place] & holds_two[place ^ bit] for place in range(SQUARE // 2) for bit in (1, 2) if place < place ^ bit]
    )
    place = jnp.stack([chip, core, lax.axis_index("rcv")]).astype(jnp.int32)

    met = flip(lax.dynamic_slice_in_dim(surface_traces, (1 - core) * side, side, axis=1), CORE)
    own_a, own_b = [], []
    for chunk in range(CHUNKS):
        here = lax.dynamic_slice_in_dim(surface_traces, core * side + chunk * rows, rows, axis=1)
        there = met[:, chunk * rows : (chunk + 1) * rows]
        own_a.append(jnp.where(mine_is_a, here, there))
        own_b.append(jnp.where(mine_is_b, here, there))

    def run(third):
        across = [flip(a, ACROSS) for a in own_a]
        down = [flip(b, DOWN) for b in own_b]

        ring = lax.axis_size("rcv")
        blocks = [primaries] + [lax.ppermute(primaries, "rcv", [(i, (i + j) % ring) for i in range(ring)]) for j in range(1, ring)]
        blocks = jnp.stack(blocks)
        blocks = jnp.concatenate([blocks, flip(blocks, CORE)], axis=1)
        blocks = jnp.pad(blocks.astype(jnp.float32), ((0, 0), (0, 0), (0, 0), (0, taps)))
        bands = bands_of(blocks, place)
        other_data = flip(lax.dynamic_slice_in_dim(data, (1 - core) * side, side, axis=1), CORE)

        across[0], down[0], bands = lax.optimization_barrier((across[0], down[0], bands))

        kept, returned = [], []
        for chunk in range(CHUNKS):
            across_again = flip(jnp.where(both, own_b[chunk], down[chunk]), ACROSS)
            down_again = flip(jnp.where(both, own_a[chunk], across[chunk]), DOWN)
            sources = [own_a[chunk], own_b[chunk], across[chunk], down[chunk], across_again, down_again]
            if third:
                sources += [flip(down_again, ACROSS), flip(across_again, DOWN)]
            mine, others = residual_of(chunk, panel_owner, place, sources, bands, data, other_data)
            kept.append(mine)
            returned.append(flip(others, CORE))
        return jnp.where(core == 0, jnp.concatenate(kept + returned, axis=1), jnp.concatenate(returned + kept, axis=1))

    return lax.cond(neighbours_full, functools.partial(run, True), functools.partial(run, False))


def solution(mesh):
    placed = (P("shot", "rcv", None), P("shot", "rcv", None), P("shot", "rcv", None), P())
    shards = square_shards if mesh.shape["shot"] == SQUARE else summed_broadcasts
    return jax.shard_map(shards, mesh=mesh, in_specs=placed, out_specs=P("shot", "rcv", None), check_vma=False)
```

```python
import functools

import jax
import jax.numpy as jnp
from jax import lax
from jax.experimental import pallas as pl
from jax.experimental.pallas import tpu as pltpu
from jax.sharding import PartitionSpec as P

CORE, ACROSS, DOWN = 1, 2, 4
SQUARE = 8
CHUNKS = 2
FIRST_SOURCES = 4
VMEM_BYTES = 20 * 1024 * 1024
SMALL_VMEM_BYTES = 2 * 1024 * 1024


def broadcast(value, axis, root):
    mine = lax.axis_index(axis) == root
    return lax.psum(jnp.where(mine, value, jnp.zeros_like(value)), axis)


def shift_table(taps, block):
    shape = (2, taps, block, block)
    lag_index, tap_index, in_index, out_index = (lax.broadcasted_iota(jnp.int32, shape, dim) for dim in range(4))
    distance = out_index - in_index + lag_index * block
    return (distance == tap_index).astype(jnp.bfloat16)


def band_matrices(panel_prim, shift_ones):
    bands = jnp.einsum("skt,ltio->lskio", panel_prim, shift_ones, preferred_element_type=jnp.float32)
    return bands.astype(jnp.bfloat16)


def convolve(traces, bands, block):
    point_count, row_count, length = traces.shape
    blocks = traces.reshape(point_count, row_count, length // block, block)
    earlier = jnp.concatenate([jnp.zeros_like(blocks[:, :, :1]), blocks[:, :, :-1]], axis=2)
    stacked = jnp.stack([blocks, earlier])
    product = jnp.einsum("lkrbi,lskio->srbo", stacked, bands, preferred_element_type=jnp.float32)
    return product.reshape(bands.shape[1], row_count, length)


def summed_broadcasts(data, surface_traces, primaries, panel_owner):
    points, taps = surface_traces.shape[0], primaries.shape[2]
    shift_ones = shift_table(taps, 2 * taps)
    summed = jnp.zeros(data.shape, jnp.float32)
    panels_here = primaries.shape[1] // points
    for panel_id in range(panel_owner.shape[0]):
        first_point = panel_id % panels_here * points
        panel_prim = broadcast(primaries, "rcv", panel_id // panels_here)[:, first_point : first_point + points]
        traces = broadcast(surface_traces, "shot", panel_owner[panel_id])
        summed = summed + convolve(traces, band_matrices(panel_prim, shift_ones), 2 * taps)
    return (data.astype(jnp.float32) - summed).astype(jnp.bfloat16)


def flip(value, bit):
    return lax.ppermute(value, "shot", [(i, i ^ bit) for i in range(SQUARE)])


def band_kernel(place_ref, taps_ref, band_ref):
    shots, points, width = taps_ref.shape[1:]
    rows = width // 2

    def point(k, carry):
        for s in range(shots):
            row = taps_ref[0, s, pl.ds(k, 1), :]
            spread = pltpu.roll(jnp.broadcast_to(row, (rows, width)), 0, 1, stride=1, stride_axis=0)
            band_ref[pl.ds(pl.multiple_of(k * rows, rows), rows), s * width : (s + 1) * width] = spread.astype(jnp.bfloat16)
        return carry

    lax.fori_loop(0, points, point, 0)


def bands_of(blocks, place):
    panels, shots, points, width = blocks.shape
    height = points * width // 2
    return pl.pallas_call(
        band_kernel,
        out_shape=jax.ShapeDtypeStruct((panels * height, shots * width), jnp.bfloat16),
        grid_spec=pltpu.PrefetchScalarGridSpec(
            num_scalar_prefetch=1,
            grid=(panels,),
            in_specs=[pl.BlockSpec((1, shots, points, width), lambda p, place: (place[2] ^ p, 0, 0, 0))],
            out_specs=pl.BlockSpec((height, shots * width), lambda p, place: (p, 0)),
        ),
        compiler_params=pltpu.CompilerParams(vmem_limit_bytes=VMEM_BYTES),
        cost_estimate=pl.CostEstimate(flops=panels * height * shots * width * 8, bytes_accessed=panels * height * shots * width * 2, transcendentals=0),
        name="bands",
    )(place, blocks)


def source_of(panel, owner_ref, chip):
    panels = owner_ref.shape[0]

    def held(place):
        count = jnp.int32(0)
        for other in range(panels):
            count = count + (owner_ref[other] // 2 == place).astype(jnp.int32)
        return count

    owner = owner_ref[panel]
    there, second = owner // 2, lax.rem(owner, 2) == 1
    both = held(there) == 2
    across_full, down_full = held(chip ^ 1) == 2, held(chip ^ 2) == 2
    own = jnp.where(both & second, 1, 0)
    across = jnp.where(both & second, 4, 2)
    down = jnp.where(both & jnp.logical_not(second), 5, 3)
    single = jnp.where(down_full, 4, 5)
    double = jnp.where(second, jnp.where(across_full, 7, 4), jnp.where(down_full, 6, 5))
    diagonal = jnp.where(both, double, single)
    return jnp.where(there == chip, own, jnp.where(there == (chip ^ 1), across, jnp.where(there == (chip ^ 2), down, diagonal)))


def plan_kernel(owner_ref, place_ref, plan_ref):
    panels = owner_ref.shape[0]
    early, late = jnp.int32(0), jnp.int32(0)
    for entry in range(3 * panels):
        plan_ref[entry] = jnp.int32(0)
    for panel in range(panels):
        source = source_of(panel, owner_ref, place_ref[0])
        plan_ref[panel] = source
        plan_ref[panels + early] = jnp.int32(panel)
        plan_ref[2 * panels + late] = jnp.int32(panel)
        met_first = source < FIRST_SOURCES
        early = early + jnp.where(met_first, 1, 0)
        late = late + jnp.where(met_first, 0, 1)
    plan_ref[3 * panels] = early
    plan_ref[3 * panels + 1] = late


def plan_of(owner, place):
    return pl.pallas_call(
        plan_kernel,
        out_shape=jax.ShapeDtypeStruct((3 * owner.shape[0] + 2,), jnp.int32),
        in_specs=[pl.BlockSpec(memory_space=pltpu.SMEM)] * 2,
        out_specs=pl.BlockSpec(memory_space=pltpu.SMEM),
        name="plan",
    )(owner, place)


def pick_kernel(chunk, owner_ref, place_ref, slot_ref, met_ref, a_ref, b_ref, sems):
    chip, core = place_ref[0], place_ref[1]
    first_owns, second_owns = jnp.bool_(False), jnp.bool_(False)
    for panel in range(owner_ref.shape[0]):
        first_owns = first_owns | (owner_ref[panel] == 2 * chip)
        second_owns = second_owns | (owner_ref[panel] == 2 * chip + 1)
    rows = met_ref.shape[1]
    start = pl.multiple_of((core * CHUNKS + chunk) * rows, rows)
    here_ref = slot_ref.at[:, pl.ds(start, rows), :]
    for index, (out_ref, mine) in enumerate(((a_ref, first_owns == (core == 0)), (b_ref, second_owns == (core == 1)))):
        @pl.when(mine)
        def _():
            pltpu.make_async_copy(here_ref, out_ref, sems.at[index]).start()

        @pl.when(jnp.logical_not(mine))
        def _():
            pltpu.make_async_copy(met_ref, out_ref, sems.at[index]).start()

    for index, out_ref in enumerate((a_ref, b_ref)):
        pltpu.make_async_copy(met_ref, out_ref, sems.at[index]).wait()


def pick(chunk, owner, place, slot, met):
    piece = jax.ShapeDtypeStruct(met.shape, met.dtype)
    return pl.pallas_call(
        functools.partial(pick_kernel, chunk),
        out_shape=(piece, piece),
        in_specs=[pl.BlockSpec(memory_space=pltpu.SMEM)] * 2 + [pl.BlockSpec(memory_space=pl.ANY)] * 2,
        out_specs=[pl.BlockSpec(memory_space=pl.ANY)] * 2,
        scratch_shapes=[pltpu.SemaphoreType.DMA((2,))],
        compiler_params=pltpu.CompilerParams(vmem_limit_bytes=SMALL_VMEM_BYTES),
        name="pick",
    )(owner, place, slot, met)


def sum_kernel(last, plan_ref, place_ref, *refs):
    extra = 5 if last else 1
    count = len(refs) - extra - 5
    sources, band_ref = refs[:count], refs[count]
    window, spread, total, arrived = refs[-4:]
    step, steps = pl.program_id(0), pl.num_programs(0)
    slots, points, rows, length = window.shape
    panels = (plan_ref.shape[0] - 2) // 3
    entries = panels * (2 if last else 1)
    wanted = plan_ref[3 * panels + (1 if last else 0)]
    half = spread.shape[1] // points
    width = 2 * half

    @pl.when(step == 0)
    def _():
        for slot in range(slots):
            chosen = jnp.clip(plan_ref[plan_ref[entries + slot]] - (FIRST_SOURCES if last else 0), 0, count - 1)
            for index, source in enumerate(sources):
                @pl.when((slot < wanted) & (chosen == index))
                def _():
                    pltpu.make_async_copy(source, window.at[slot], arrived.at[slot]).start()

    low = lax.broadcasted_iota(jnp.int32, (rows, width), 1) < half

    @pl.when(step < wanted)
    def _():
        pltpu.make_async_copy(sources[0], window.at[step], arrived.at[step]).wait()
        for j in range(points // 2):
            for c in range(length // width):
                first = window[step, 2 * j, :, c * width : (c + 1) * width].astype(jnp.float32)
                second = window[step, 2 * j + 1, :, c * width : (c + 1) * width].astype(jnp.float32)
                even = jnp.where(low, first, pltpu.roll(second, half, 1))
                odd = jnp.where(low, pltpu.roll(first, half, 1), second)
                spread[2 * c * rows : (2 * c + 1) * rows, j * width : (j + 1) * width] = even.astype(jnp.bfloat16)
                spread[(2 * c + 1) * rows : (2 * c + 2) * rows, j * width : (j + 1) * width] = odd.astype(jnp.bfloat16)
        product = jnp.dot(spread[...], band_ref[...], preferred_element_type=jnp.float32)

        @pl.when(step == 0)
        def _():
            total[...] = product

        @pl.when(step > 0)
        def _():
            total[...] += product

    @pl.when((step == 0) & (wanted == 0))
    def _():
        total[...] = jnp.zeros_like(total)

    @pl.when(step == steps - 1)
    def _():
        for s in range(total.shape[1] // width):

            def part(b):
                return total[b * rows : (b + 1) * rows, s * width : (s + 1) * width]

            for c in range(length // width):
                before = part(2 * c - 1) if c > 0 else jnp.zeros((rows, width), jnp.float32)
                summed = part(2 * c) + pltpu.roll(jnp.where(low, part(2 * c + 1), before), half, 1)
                span = slice(c * width, (c + 1) * width)
                if last:
                    early_ref, mine_ref, other_ref, out_mine_ref, out_other_ref = refs[count + 1 : -4]
                    shots = mine_ref.shape[0]
                    data_ref, out_ref = (mine_ref, out_mine_ref) if s < shots else (other_ref, out_other_ref)
                    summed = summed + early_ref[s, :, span]
                    here = data_ref[s % shots, :, span].astype(jnp.float32)
                    out_ref[s % shots, :, span] = (here - summed).astype(jnp.bfloat16)
                else:
                    refs[count + 1][s, :, span] = summed


def sum_of(plan, place, sources, bands, steps, taps, late=None):
    points, rows, length = sources[0].shape
    panels = (plan.shape[0] - 2) // 3
    height, columns = bands.shape[0] // panels, bands.shape[1]
    shots = columns // (2 * taps)
    last = late is not None
    entries = panels * (2 if last else 1)

    def band_place(step, plan, place):
        wanted = plan[3 * panels + (1 if last else 0)]
        return (plan[entries + jnp.maximum(jnp.minimum(step, wanted - 1), 0)], 0)

    in_specs = [pl.BlockSpec(memory_space=pl.ANY)] * len(sources) + [pl.BlockSpec((height, columns), band_place)]
    operands = [*sources, bands]
    if last:
        chunk, early, data, other_data = late
        half = shots // 2
        piece = jax.ShapeDtypeStruct((half, rows, length), jnp.bfloat16)
        in_specs += [
            pl.BlockSpec((shots, rows, length), lambda step, plan, place: (0, 0, 0)),
            pl.BlockSpec((half, rows, length), lambda step, plan, place: (0, place[1] * CHUNKS + chunk, 0)),
            pl.BlockSpec((half, rows, length), lambda step, plan, place: (0, chunk, 0)),
        ]
        operands += [early, data, other_data]
        out_shape = (piece, piece)
        out_specs = [pl.BlockSpec((half, rows, length), lambda step, plan, place: (0, 0, 0))] * 2
    else:
        out_shape = jax.ShapeDtypeStruct((shots, rows, length), jnp.float32)
        out_specs = pl.BlockSpec((shots, rows, length), lambda step, plan, place: (0, 0, 0))
    tall = rows * length // taps
    return pl.pallas_call(
        functools.partial(sum_kernel, last),
        out_shape=out_shape,
        grid_spec=pltpu.PrefetchScalarGridSpec(
            num_scalar_prefetch=2,
            grid=(steps,),
            in_specs=in_specs,
            out_specs=out_specs,
            scratch_shapes=[
                pltpu.VMEM((steps, points, rows, length), jnp.bfloat16),
                pltpu.VMEM((tall, height), jnp.bfloat16),
                pltpu.VMEM((tall, columns), jnp.float32),
                pltpu.SemaphoreType.DMA((steps,)),
            ],
        ),
        compiler_params=pltpu.CompilerParams(vmem_limit_bytes=VMEM_BYTES),
        cost_estimate=pl.CostEstimate(flops=2 * tall * steps * height * columns, bytes_accessed=2 * steps * height * columns, transcendentals=0),
        name="residual" if last else "early_sum",
    )(plan, place, *operands)


def assemble_kernel(place_ref, *refs):
    pieces, out_ref, sems = refs[:-2], refs[-2], refs[-1]
    rows = pieces[0].shape[1]
    copies = []
    for index, piece in enumerate(pieces):
        side = place_ref[1] if index < CHUNKS else 1 - place_ref[1]
        start = pl.multiple_of((side * CHUNKS + index % CHUNKS) * rows, rows)
        copies.append(pltpu.make_async_copy(piece, out_ref.at[:, pl.ds(start, rows), :], sems.at[index]))
    for copy in copies:
        copy.start()
    for copy in copies:
        copy.wait()


def assemble(place, pieces, like):
    return pl.pallas_call(
        assemble_kernel,
        out_shape=jax.ShapeDtypeStruct(like.shape, like.dtype),
        in_specs=[pl.BlockSpec(memory_space=pltpu.SMEM)] + [pl.BlockSpec(memory_space=pl.ANY)] * len(pieces),
        out_specs=pl.BlockSpec(memory_space=pl.ANY),
        scratch_shapes=[pltpu.SemaphoreType.DMA((len(pieces),))],
        compiler_params=pltpu.CompilerParams(vmem_limit_bytes=SMALL_VMEM_BYTES),
        name="assemble",
    )(place, *pieces)


def square_shards(data, surface_traces, primaries, panel_owner):
    panels = panel_owner.shape[0]
    side = data.shape[1] // 2
    rows = side // CHUNKS
    taps = primaries.shape[2]
    me = lax.axis_index("shot")
    core, chip = me % 2, me // 2
    place = jnp.stack([chip, core, lax.axis_index("rcv")]).astype(jnp.int32)
    holds_two = [jnp.sum(panel_owner // 2 == other) == 2 for other in range(SQUARE // 2)]
    both = jnp.sum(panel_owner // 2 == chip) == 2
    neighbours_full = functools.reduce(
        jnp.logical_or, [holds_two[at] & holds_two[at ^ bit] for at in range(SQUARE // 2) for bit in (1, 2) if at < at ^ bit]
    )

    own_a, own_b, across, down = [], [], [], []
    for chunk in range(CHUNKS):
        there = lax.dynamic_slice_in_dim(surface_traces, (1 - core) * side + chunk * rows, rows, axis=1)
        a, b = pick(chunk, panel_owner, place, surface_traces, flip(there, CORE))
        own_a.append(a)
        own_b.append(b)
        across.append(flip(a, ACROSS))
        down.append(flip(b, DOWN))

    own_a[-1], primaries, data_there = lax.optimization_barrier((own_a[-1], primaries, data))
    ring = lax.axis_size("rcv")
    blocks, bit = primaries[None], 1
    while bit < ring:
        blocks = jnp.concatenate([blocks, lax.ppermute(blocks, "rcv", [(i, i ^ bit) for i in range(ring)])])
        bit *= 2
    blocks = jnp.concatenate([blocks, flip(blocks, CORE)], axis=1)
    blocks = jnp.pad(blocks.astype(jnp.float32), ((0, 0), (0, 0), (0, 0), (0, taps)))
    bands = bands_of(blocks, place)
    plan = plan_of(panel_owner, place)
    other_data = flip(lax.dynamic_slice_in_dim(data_there, (1 - core) * side, side, axis=1), CORE)
    across[0], down[0], bands = lax.optimization_barrier((across[0], down[0], bands))

    sources, early = [], []
    for chunk in range(CHUNKS):
        across_again = flip(jnp.where(both, own_b[chunk], down[chunk]), ACROSS)
        down_again = flip(jnp.where(both, own_a[chunk], across[chunk]), DOWN)
        first = [own_a[chunk], own_b[chunk], across[chunk], down[chunk]]
        early.append(sum_of(plan, place, first, bands, panels, taps))
        sources.append([across_again, down_again])

    def finish(sources, steps):
        kept, returned = [], []
        for chunk in range(CHUNKS):
            mine, others = sum_of(plan, place, sources[chunk], bands, steps, taps, (chunk, early[chunk], data, other_data))
            kept.append(mine)
            returned.append(flip(others, CORE))
        return assemble(place, kept + returned, data)

    def third_step():
        return finish([[a, d, flip(d, ACROSS), flip(a, DOWN)] for a, d in sources], panels - 1)

    residual = finish(sources, 2)
    return lax.cond(neighbours_full, third_step, lambda: residual)


def solution(mesh):
    placed = (P("shot", "rcv", None), P("shot", "rcv", None), P("shot", "rcv", None), P())
    shards = square_shards if mesh.shape["shot"] == SQUARE else summed_broadcasts
    return jax.shard_map(shards, mesh=mesh, in_specs=placed, out_specs=P("shot", "rcv", None), check_vma=False)
```

```python
import functools

import jax
import jax.numpy as jnp
from jax import lax
from jax.experimental import pallas as pl
from jax.experimental.pallas import tpu as pltpu
from jax.sharding import PartitionSpec as P

CORE, ACROSS, DOWN = 1, 2, 4
SQUARE = 8
CHUNKS = 2
FIRST_SOURCES = 4
VMEM_BYTES = 16 * 1024 * 1024
SMALL_VMEM_BYTES = 2 * 1024 * 1024
IN_SMEM = pl.BlockSpec(memory_space=pltpu.SMEM)
ANYWHERE = pl.BlockSpec(memory_space=pl.ANY)
NO_COST = pl.CostEstimate(flops=0, bytes_accessed=0, transcendentals=0)


def broadcast(value, axis, root):
    mine = lax.axis_index(axis) == root
    return lax.psum(jnp.where(mine, value, jnp.zeros_like(value)), axis)


def shift_table(taps, block):
    shape = (2, taps, block, block)
    lag_index, tap_index, in_index, out_index = (lax.broadcasted_iota(jnp.int32, shape, dim) for dim in range(4))
    distance = out_index - in_index + lag_index * block
    return (distance == tap_index).astype(jnp.bfloat16)


def band_matrices(panel_prim, shift_ones):
    bands = jnp.einsum("skt,ltio->lskio", panel_prim, shift_ones, preferred_element_type=jnp.float32)
    return bands.astype(jnp.bfloat16)


def convolve(traces, bands, block):
    point_count, row_count, length = traces.shape
    blocks = traces.reshape(point_count, row_count, length // block, block)
    earlier = jnp.concatenate([jnp.zeros_like(blocks[:, :, :1]), blocks[:, :, :-1]], axis=2)
    stacked = jnp.stack([blocks, earlier])
    product = jnp.einsum("lkrbi,lskio->srbo", stacked, bands, preferred_element_type=jnp.float32)
    return product.reshape(bands.shape[1], row_count, length)


def summed_broadcasts(data, surface_traces, primaries, panel_owner):
    points, taps = surface_traces.shape[0], primaries.shape[2]
    shift_ones = shift_table(taps, 2 * taps)
    summed = jnp.zeros(data.shape, jnp.float32)
    panels_here = primaries.shape[1] // points
    for panel_id in range(panel_owner.shape[0]):
        first_point = panel_id % panels_here * points
        panel_prim = broadcast(primaries, "rcv", panel_id // panels_here)[:, first_point : first_point + points]
        traces = broadcast(surface_traces, "shot", panel_owner[panel_id])
        summed = summed + convolve(traces, band_matrices(panel_prim, shift_ones), 2 * taps)
    return (data.astype(jnp.float32) - summed).astype(jnp.bfloat16)


def flip(value, bit):
    return lax.ppermute(value, "shot", [(i, i ^ bit) for i in range(SQUARE)])


def band_kernel(place_ref, taps_ref, band_ref):
    shots, points, width = taps_ref.shape[1:]
    rows = width // 2

    def point(k, carry):
        for s in range(shots):
            row = taps_ref[0, s, pl.ds(k, 1), :]
            spread = pltpu.roll(jnp.broadcast_to(row, (rows, width)), 0, 1, stride=1, stride_axis=0)
            band_ref[pl.ds(pl.multiple_of(k * rows, rows), rows), s * width : (s + 1) * width] = spread.astype(jnp.bfloat16)
        return carry

    lax.fori_loop(0, points, point, 0)


def bands_of(blocks, place):
    panels, shots, points, width = blocks.shape
    height = points * width // 2
    return pl.pallas_call(
        band_kernel,
        out_shape=jax.ShapeDtypeStruct((panels * height, shots * width), jnp.bfloat16),
        grid_spec=pltpu.PrefetchScalarGridSpec(
            num_scalar_prefetch=1,
            grid=(panels,),
            in_specs=[pl.BlockSpec((1, shots, points, width), lambda p, place: (place[2] ^ p, 0, 0, 0))],
            out_specs=pl.BlockSpec((height, shots * width), lambda p, place: (p, 0)),
        ),
        compiler_params=pltpu.CompilerParams(vmem_limit_bytes=VMEM_BYTES),
        cost_estimate=pl.CostEstimate(flops=panels * height * shots * width * 8, bytes_accessed=panels * height * shots * width * 2, transcendentals=0),
        name="bands",
    )(place, blocks)


def source_of(panel, owner_ref, chip):
    panels = owner_ref.shape[0]

    def held(place):
        count = jnp.int32(0)
        for other in range(panels):
            count = count + (owner_ref[other] // 2 == place).astype(jnp.int32)
        return count

    owner = owner_ref[panel]
    there, second = owner // 2, lax.rem(owner, 2) == 1
    both = held(there) == 2
    across_full, down_full = held(chip ^ 1) == 2, held(chip ^ 2) == 2
    own = jnp.where(both & second, 1, 0)
    across = jnp.where(both & second, 4, 2)
    down = jnp.where(both & jnp.logical_not(second), 5, 3)
    single = jnp.where(down_full, 4, 5)
    double = jnp.where(second, jnp.where(across_full, 7, 4), jnp.where(down_full, 6, 5))
    diagonal = jnp.where(both, double, single)
    return jnp.where(there == chip, own, jnp.where(there == (chip ^ 1), across, jnp.where(there == (chip ^ 2), down, diagonal)))


def plan_kernel(owner_ref, place_ref, plan_ref):
    panels = owner_ref.shape[0]
    early, late = jnp.int32(0), jnp.int32(0)
    for entry in range(3 * panels):
        plan_ref[entry] = jnp.int32(0)
    for panel in range(panels):
        source = source_of(panel, owner_ref, place_ref[0])
        plan_ref[panel] = source
        plan_ref[panels + early] = jnp.int32(panel)
        plan_ref[2 * panels + late] = jnp.int32(panel)
        met_first = source < FIRST_SOURCES
        early = early + jnp.where(met_first, 1, 0)
        late = late + jnp.where(met_first, 0, 1)
    plan_ref[3 * panels] = early
    plan_ref[3 * panels + 1] = late


def plan_of(owner, place):
    return pl.pallas_call(
        plan_kernel,
        out_shape=jax.ShapeDtypeStruct((3 * owner.shape[0] + 2,), jnp.int32),
        in_specs=[pl.BlockSpec(memory_space=pltpu.SMEM)] * 2,
        out_specs=pl.BlockSpec(memory_space=pltpu.SMEM),
        cost_estimate=NO_COST,
        name="plan",
    )(owner, place)


def pick_kernel(passed, before, owner_ref, place_ref, slot_ref, met_ref, *refs):
    chip, core = place_ref[0], place_ref[1]
    first_owns, second_owns = jnp.bool_(False), jnp.bool_(False)
    for panel in range(owner_ref.shape[0]):
        first_owns = first_owns | (owner_ref[panel] == 2 * chip)
        second_owns = second_owns | (owner_ref[panel] == 2 * chip + 1)
    outs, sems = refs[passed + before : -1], refs[-1]
    points, rows, _ = outs[0].shape
    shots = met_ref.shape[0] - points
    for chunk in range(CHUNKS):
        here_ref = slot_ref.at[:, pl.ds(pl.multiple_of((core * CHUNKS + chunk) * rows, rows), rows), :]
        there_ref = met_ref.at[pl.ds(shots, points), pl.ds(chunk * rows, rows), :]
        for which, mine in enumerate((first_owns == (core == 0), second_owns == (core == 1))):
            index = 2 * chunk + which

            @pl.when(mine)
            def _():
                pltpu.make_async_copy(here_ref, outs[index], sems.at[index]).start()

            @pl.when(jnp.logical_not(mine))
            def _():
                pltpu.make_async_copy(there_ref, outs[index], sems.at[index]).start()

    copies = [pltpu.make_async_copy(refs[index], outs[2 * CHUNKS + index], sems.at[2 * CHUNKS + index]) for index in range(passed)]
    for copy in copies:
        copy.start()
    for index in range(2 * CHUNKS):
        pltpu.make_async_copy(met_ref.at[pl.ds(shots, points), pl.ds(0, rows), :], outs[index], sems.at[index]).wait()
    for copy in copies:
        copy.wait()


def pick(owner, place, slot, met, passed, before):
    points, side, length = slot.shape[0], met.shape[1], met.shape[2]
    outs = [jax.ShapeDtypeStruct((points, side // CHUNKS, length), met.dtype)] * (2 * CHUNKS)
    outs += [jax.ShapeDtypeStruct(value.shape, value.dtype) for value in passed]
    outs = pl.pallas_call(
        functools.partial(pick_kernel, len(passed), len(before)),
        out_shape=tuple(outs),
        in_specs=[IN_SMEM] * 2 + [ANYWHERE] * (2 + len(passed) + len(before)),
        out_specs=[ANYWHERE] * len(outs),
        scratch_shapes=[pltpu.SemaphoreType.DMA((len(outs),))],
        compiler_params=pltpu.CompilerParams(vmem_limit_bytes=SMALL_VMEM_BYTES),
        cost_estimate=NO_COST,
        name="pick",
    )(owner, place, slot, met, *passed, *before)
    return outs[0 : 2 * CHUNKS : 2], outs[1 : 2 * CHUNKS : 2], *outs[2 * CHUNKS :]


def sum_kernel(last, plan_ref, place_ref, *refs):
    extra = 5 if last else 1
    count = len(refs) - extra - 5
    sources, band_ref = refs[:count], refs[count]
    window, spread, total, arrived = refs[-4:]
    step, steps = pl.program_id(0), pl.num_programs(0)
    slots, points, rows, length = window.shape
    panels = (plan_ref.shape[0] - 2) // 3
    entries = panels * (2 if last else 1)
    wanted = plan_ref[3 * panels + (1 if last else 0)]
    half = spread.shape[1] // points
    width = 2 * half

    @pl.when(step == 0)
    def _():
        for slot in range(slots):
            chosen = jnp.clip(plan_ref[plan_ref[entries + slot]] - (FIRST_SOURCES if last else 0), 0, count - 1)
            for index, source in enumerate(sources):
                @pl.when((slot < wanted) & (chosen == index))
                def _():
                    pltpu.make_async_copy(source, window.at[slot], arrived.at[slot]).start()

    low = lax.broadcasted_iota(jnp.int32, (rows, width), 1) < half

    @pl.when(step < wanted)
    def _():
        pltpu.make_async_copy(sources[0], window.at[step], arrived.at[step]).wait()
        for j in range(points // 2):
            for c in range(length // width):
                first = window[step, 2 * j, :, c * width : (c + 1) * width].astype(jnp.float32)
                second = window[step, 2 * j + 1, :, c * width : (c + 1) * width].astype(jnp.float32)
                even = jnp.where(low, first, pltpu.roll(second, half, 1))
                odd = jnp.where(low, pltpu.roll(first, half, 1), second)
                spread[2 * c * rows : (2 * c + 1) * rows, j * width : (j + 1) * width] = even.astype(jnp.bfloat16)
                spread[(2 * c + 1) * rows : (2 * c + 2) * rows, j * width : (j + 1) * width] = odd.astype(jnp.bfloat16)
        product = jnp.dot(spread[...], band_ref[...], preferred_element_type=jnp.float32)

        @pl.when(step == 0)
        def _():
            total[...] = product

        @pl.when(step > 0)
        def _():
            total[...] += product

    @pl.when((step == 0) & (wanted == 0))
    def _():
        total[...] = jnp.zeros_like(total)

    @pl.when(step == steps - 1)
    def _():
        for s in range(total.shape[1] // width):

            def part(b):
                return total[b * rows : (b + 1) * rows, s * width : (s + 1) * width]

            for c in range(length // width):
                before = part(2 * c - 1) if c > 0 else jnp.zeros((rows, width), jnp.float32)
                summed = part(2 * c) + pltpu.roll(jnp.where(low, part(2 * c + 1), before), half, 1)
                span = slice(c * width, (c + 1) * width)
                if last:
                    early_ref, mine_ref, other_ref, out_mine_ref, out_other_ref = refs[count + 1 : -4]
                    shots = mine_ref.shape[0]
                    data_ref, out_ref = (mine_ref, out_mine_ref) if s < shots else (other_ref, out_other_ref)
                    summed = summed + early_ref[s, :, span]
                    here = data_ref[s % shots, :, span].astype(jnp.float32)
                    out_ref[s % shots, :, span] = (here - summed).astype(jnp.bfloat16)
                else:
                    refs[count + 1][s, :, span] = summed


def sum_of(plan, place, sources, bands, steps, taps, late=None):
    points, rows, length = sources[0].shape
    panels = (plan.shape[0] - 2) // 3
    height, columns = bands.shape[0] // panels, bands.shape[1]
    shots = columns // (2 * taps)
    last = late is not None
    entries = panels * (2 if last else 1)

    def band_place(step, plan, place):
        wanted = plan[3 * panels + (1 if last else 0)]
        return (plan[entries + jnp.maximum(jnp.minimum(step, wanted - 1), 0)], 0)

    in_specs = [ANYWHERE] * len(sources) + [pl.BlockSpec((height, columns), band_place)]
    operands = [*sources, bands]
    if last:
        chunk, early, data, other_data = late
        half = shots // 2
        piece = jax.ShapeDtypeStruct((half, rows, length), jnp.bfloat16)
        in_specs += [
            pl.BlockSpec((shots, rows, length), lambda step, plan, place: (0, 0, 0)),
            pl.BlockSpec((half, rows, length), lambda step, plan, place: (0, place[1] * CHUNKS + chunk, 0)),
            pl.BlockSpec((half, rows, length), lambda step, plan, place: (0, chunk, 0)),
        ]
        operands += [early, data, other_data]
        out_shape = (piece, piece)
        out_specs = [pl.BlockSpec((half, rows, length), lambda step, plan, place: (0, 0, 0))] * 2
    else:
        out_shape = jax.ShapeDtypeStruct((shots, rows, length), jnp.float32)
        out_specs = pl.BlockSpec((shots, rows, length), lambda step, plan, place: (0, 0, 0))
    tall = rows * length // taps
    return pl.pallas_call(
        functools.partial(sum_kernel, last),
        out_shape=out_shape,
        grid_spec=pltpu.PrefetchScalarGridSpec(
            num_scalar_prefetch=2,
            grid=(steps,),
            in_specs=in_specs,
            out_specs=out_specs,
            scratch_shapes=[
                pltpu.VMEM((steps, points, rows, length), jnp.bfloat16),
                pltpu.VMEM((tall, height), jnp.bfloat16),
                pltpu.VMEM((tall, columns), jnp.float32),
                pltpu.SemaphoreType.DMA((steps,)),
            ],
        ),
        compiler_params=pltpu.CompilerParams(vmem_limit_bytes=VMEM_BYTES),
        cost_estimate=pl.CostEstimate(flops=2 * tall * steps * height * columns, bytes_accessed=2 * steps * height * columns, transcendentals=0),
        name="residual" if last else "early_sum",
    )(plan, place, *operands)


def assemble_kernel(place_ref, *refs):
    pieces, out_ref, sems = refs[:-2], refs[-2], refs[-1]
    rows = pieces[0].shape[1]
    copies = []
    for index, piece in enumerate(pieces):
        side = place_ref[1] if index < CHUNKS else 1 - place_ref[1]
        start = pl.multiple_of((side * CHUNKS + index % CHUNKS) * rows, rows)
        copies.append(pltpu.make_async_copy(piece, out_ref.at[:, pl.ds(start, rows), :], sems.at[index]))
    for copy in copies:
        copy.start()
    for copy in copies:
        copy.wait()


def assemble(place, pieces, like):
    return pl.pallas_call(
        assemble_kernel,
        out_shape=jax.ShapeDtypeStruct(like.shape, like.dtype),
        in_specs=[IN_SMEM] + [pl.BlockSpec(memory_space=pl.ANY)] * len(pieces),
        out_specs=ANYWHERE,
        scratch_shapes=[pltpu.SemaphoreType.DMA((len(pieces),))],
        compiler_params=pltpu.CompilerParams(vmem_limit_bytes=SMALL_VMEM_BYTES),
        cost_estimate=NO_COST,
        name="assemble",
    )(place, *pieces)


def any_of(flags):
    return functools.reduce(jnp.logical_or, flags)


def exchange(data, surface_traces, primaries, panel_owner, place, third):
    panels = panel_owner.shape[0]
    side = data.shape[1] // 2
    rows = side // CHUNKS
    taps = primaries.shape[2]
    core = lax.rem(lax.axis_index("shot"), 2)
    plan = plan_of(panel_owner, place)
    ring = lax.axis_size("rcv")
    there = jnp.concatenate([lax.dynamic_slice_in_dim(array, (1 - core) * side, side, axis=1) for array in (data, surface_traces)])
    met = flip(there, CORE)
    ahead = lax.ppermute(primaries, "rcv", [(i, i ^ 1) for i in range(ring)])
    own_a, own_b, primaries = pick(panel_owner, place, surface_traces, met, (primaries,), (ahead,))
    across, down = [flip(a, ACROSS) for a in own_a], [flip(b, DOWN) for b in own_b]
    blocks, bit = jnp.stack([primaries, ahead]), 2
    while bit < ring:
        blocks = jnp.concatenate([blocks, lax.ppermute(blocks, "rcv", [(i, i ^ bit) for i in range(ring)])])
        bit *= 2
    blocks = jnp.concatenate([blocks, flip(blocks, CORE)], axis=1)
    blocks = jnp.pad(blocks.astype(jnp.float32), ((0, 0), (0, 0), (0, 0), (0, taps)))
    bands = bands_of(blocks, place)
    both = jnp.sum(panel_owner // 2 == place[0]) == 2
    for_across = [jnp.where(both, own_b[chunk], down[chunk]) for chunk in range(CHUNKS)]
    for_down = [jnp.where(both, own_a[chunk], across[chunk]) for chunk in range(CHUNKS)]

    kept, returned = [], []
    for chunk in range(CHUNKS):
        first = [own_a[chunk], own_b[chunk], across[chunk], down[chunk]]
        second = [flip(for_across[chunk], ACROSS), flip(for_down[chunk], DOWN)]
        if third:
            second += [flip(second[1], ACROSS), flip(second[0], DOWN)]
        early = sum_of(plan, place, first, bands, panels, taps)
        mine, others = sum_of(plan, place, second, bands, panels - 1 if third else 2, taps, (chunk, early, data, met))
        kept.append(mine)
        returned.append(flip(others, CORE))
    return assemble(place, kept + returned, data)


def square_shards(data, surface_traces, primaries, panel_owner):
    me = lax.axis_index("shot")
    place = jnp.stack([me // 2, me % 2, lax.axis_index("rcv")]).astype(jnp.int32)
    holds_two = [jnp.sum(panel_owner // 2 == other) == 2 for other in range(SQUARE // 2)]
    neighbours_full = any_of([holds_two[at] & holds_two[at ^ bit] for at in range(SQUARE // 2) for bit in (1, 2) if at < at ^ bit])
    arguments = (data, surface_traces, primaries, panel_owner, place)
    residual = exchange(*arguments, False)
    return lax.while_loop(lambda state: state[0], lambda state: (jnp.bool_(False), exchange(*arguments, True)), (neighbours_full, residual))[1]


def solution(mesh):
    placed = (P("shot", "rcv", None), P("shot", "rcv", None), P("shot", "rcv", None), P())
    shards = square_shards if mesh.shape["shot"] == SQUARE else summed_broadcasts
    return jax.shard_map(shards, mesh=mesh, in_specs=placed, out_specs=P("shot", "rcv", None), check_vma=False)
```

```python
import functools

import jax
import jax.numpy as jnp
from jax import lax
from jax.experimental import pallas as pl
from jax.experimental.pallas import tpu as pltpu
from jax.sharding import PartitionSpec as P

CORE, ACROSS, DOWN = 1, 2, 4
SQUARE = 8
CHUNKS = 2
FIRST_SOURCES = 4
VMEM_BYTES = 16 * 1024 * 1024
SMALL_VMEM_BYTES = 2 * 1024 * 1024
IN_SMEM = pl.BlockSpec(memory_space=pltpu.SMEM)
ANYWHERE = pl.BlockSpec(memory_space=pl.ANY)
NO_COST = pl.CostEstimate(flops=0, bytes_accessed=0, transcendentals=0)


def broadcast(value, axis, root):
    mine = lax.axis_index(axis) == root
    return lax.psum(jnp.where(mine, value, jnp.zeros_like(value)), axis)


def shift_table(taps, block):
    shape = (2, taps, block, block)
    lag_index, tap_index, in_index, out_index = (lax.broadcasted_iota(jnp.int32, shape, dim) for dim in range(4))
    distance = out_index - in_index + lag_index * block
    return (distance == tap_index).astype(jnp.bfloat16)


def band_matrices(panel_prim, shift_ones):
    bands = jnp.einsum("skt,ltio->lskio", panel_prim, shift_ones, preferred_element_type=jnp.float32)
    return bands.astype(jnp.bfloat16)


def convolve(traces, bands, block):
    point_count, row_count, length = traces.shape
    blocks = traces.reshape(point_count, row_count, length // block, block)
    earlier = jnp.concatenate([jnp.zeros_like(blocks[:, :, :1]), blocks[:, :, :-1]], axis=2)
    stacked = jnp.stack([blocks, earlier])
    product = jnp.einsum("lkrbi,lskio->srbo", stacked, bands, preferred_element_type=jnp.float32)
    return product.reshape(bands.shape[1], row_count, length)


def summed_broadcasts(data, surface_traces, primaries, panel_owner):
    points, taps = surface_traces.shape[0], primaries.shape[2]
    shift_ones = shift_table(taps, 2 * taps)
    summed = jnp.zeros(data.shape, jnp.float32)
    panels_here = primaries.shape[1] // points
    for panel_id in range(panel_owner.shape[0]):
        first_point = panel_id % panels_here * points
        panel_prim = broadcast(primaries, "rcv", panel_id // panels_here)[:, first_point : first_point + points]
        traces = broadcast(surface_traces, "shot", panel_owner[panel_id])
        summed = summed + convolve(traces, band_matrices(panel_prim, shift_ones), 2 * taps)
    return (data.astype(jnp.float32) - summed).astype(jnp.bfloat16)


def flip(value, bit):
    return lax.ppermute(value, "shot", [(i, i ^ bit) for i in range(SQUARE)])


def band_kernel(place_ref, taps_ref, full_ref, band_ref, full_out_ref):
    shots, points, width = taps_ref.shape[1:]
    rows = width // 2

    def point(k, carry):
        for s in range(shots):
            row = taps_ref[0, s, pl.ds(k, 1), :]
            spread = pltpu.roll(jnp.broadcast_to(row, (rows, width)), 0, 1, stride=1, stride_axis=0)
            band_ref[pl.ds(pl.multiple_of(k * rows, rows), rows), s * width : (s + 1) * width] = spread.astype(jnp.bfloat16)
        return carry

    lax.fori_loop(0, points, point, 0)
    full_out_ref[...] = full_ref[...]


def bands_of(blocks, place, full):
    panels, shots, points, width = blocks.shape
    height = points * width // 2
    row = pl.BlockSpec(full.shape, lambda p, place: (0, 0))
    return pl.pallas_call(
        band_kernel,
        out_shape=(jax.ShapeDtypeStruct((panels * height, shots * width), jnp.bfloat16), jax.ShapeDtypeStruct(full.shape, full.dtype)),
        grid_spec=pltpu.PrefetchScalarGridSpec(
            num_scalar_prefetch=1,
            grid=(panels,),
            in_specs=[pl.BlockSpec((1, shots, points, width), lambda p, place: (place[2] ^ p, 0, 0, 0)), row],
            out_specs=[pl.BlockSpec((height, shots * width), lambda p, place: (p, 0)), row],
        ),
        compiler_params=pltpu.CompilerParams(vmem_limit_bytes=VMEM_BYTES),
        cost_estimate=pl.CostEstimate(flops=panels * height * shots * width * 8, bytes_accessed=panels * height * shots * width * 2, transcendentals=0),
        name="bands",
    )(place, blocks, full)


def source_of(panel, owner_ref, chip):
    panels = owner_ref.shape[0]

    def held(place):
        count = jnp.int32(0)
        for other in range(panels):
            count = count + (owner_ref[other] // 2 == place).astype(jnp.int32)
        return count

    owner = owner_ref[panel]
    there, second = owner // 2, lax.rem(owner, 2) == 1
    both = held(there) == 2
    across_full, down_full = held(chip ^ 1) == 2, held(chip ^ 2) == 2
    own = jnp.where(both & second, 1, 0)
    across = jnp.where(both & second, 4, 2)
    down = jnp.where(both & jnp.logical_not(second), 5, 3)
    single = jnp.where(down_full, 4, 5)
    double = jnp.where(second, jnp.where(across_full, 7, 4), jnp.where(down_full, 6, 5))
    diagonal = jnp.where(both, double, single)
    return jnp.where(there == chip, own, jnp.where(there == (chip ^ 1), across, jnp.where(there == (chip ^ 2), down, diagonal)))


def plan_kernel(owner_ref, place_ref, plan_ref, full_ref):
    panels = owner_ref.shape[0]
    early, late = jnp.int32(0), jnp.int32(0)
    for entry in range(3 * panels):
        plan_ref[entry] = jnp.int32(0)
    for panel in range(panels):
        source = source_of(panel, owner_ref, place_ref[0])
        plan_ref[panel] = source
        plan_ref[panels + early] = jnp.int32(panel)
        plan_ref[2 * panels + late] = jnp.int32(panel)
        met_first = source < FIRST_SOURCES
        early = early + jnp.where(met_first, 1, 0)
        late = late + jnp.where(met_first, 0, 1)
    plan_ref[3 * panels] = early
    plan_ref[3 * panels + 1] = late
    here = jnp.int32(0)
    for panel in range(panels):
        here = here + (owner_ref[panel] // 2 == place_ref[0]).astype(jnp.int32)
    full_ref[...] = jnp.full(full_ref.shape, jnp.where(here == 2, 1.0, 0.0), jnp.float32)


def plan_of(owner, place, length):
    return pl.pallas_call(
        plan_kernel,
        out_shape=(jax.ShapeDtypeStruct((3 * owner.shape[0] + 2,), jnp.int32), jax.ShapeDtypeStruct((1, length), jnp.float32)),
        in_specs=[IN_SMEM] * 2,
        out_specs=[IN_SMEM, pl.BlockSpec(memory_space=pltpu.VMEM)],
        cost_estimate=NO_COST,
        name="plan",
    )(owner, place)


def pick_kernel(chunk, owner_ref, place_ref, slot_ref, met_ref, *refs):
    chip, core = place_ref[0], place_ref[1]
    first_owns, second_owns = jnp.bool_(False), jnp.bool_(False)
    for panel in range(owner_ref.shape[0]):
        first_owns = first_owns | (owner_ref[panel] == 2 * chip)
        second_owns = second_owns | (owner_ref[panel] == 2 * chip + 1)
    outs, sems = refs[-3:-1], refs[-1]
    points, rows, _ = outs[0].shape
    here_ref = slot_ref.at[:, pl.ds(pl.multiple_of((core * CHUNKS + chunk) * rows, rows), rows), :]
    there_ref = met_ref.at[pl.ds(0, points), pl.ds(chunk * rows, rows), :]
    for index, mine in enumerate((first_owns == (core == 0), second_owns == (core == 1))):
        @pl.when(mine)
        def _():
            pltpu.make_async_copy(here_ref, outs[index], sems.at[index]).start()

        @pl.when(jnp.logical_not(mine))
        def _():
            pltpu.make_async_copy(there_ref, outs[index], sems.at[index]).start()

    for index in range(2):
        pltpu.make_async_copy(there_ref, outs[index], sems.at[index]).wait()


def pick(chunk, owner, place, slot, met, before):
    piece = jax.ShapeDtypeStruct((slot.shape[0], met.shape[1] // CHUNKS, slot.shape[2]), slot.dtype)
    return pl.pallas_call(
        functools.partial(pick_kernel, chunk),
        out_shape=(piece, piece),
        in_specs=[IN_SMEM] * 2 + [ANYWHERE] * (2 + len(before)),
        out_specs=[pl.BlockSpec(memory_space=pltpu.VMEM)] * 2,
        scratch_shapes=[pltpu.SemaphoreType.DMA((2,))],
        compiler_params=pltpu.CompilerParams(vmem_limit_bytes=2 * SMALL_VMEM_BYTES),
        cost_estimate=NO_COST,
        name="pick",
    )(owner, place, slot, met, *before)


def hand_on_kernel(value_ref, *refs):
    refs[-1][...] = value_ref[...]


def hand_on(value, before):
    whole = pl.BlockSpec(memory_space=pltpu.VMEM)
    return pl.pallas_call(
        hand_on_kernel,
        out_shape=jax.ShapeDtypeStruct(value.shape, value.dtype),
        in_specs=[whole] + [ANYWHERE] * len(before),
        out_specs=whole,
        compiler_params=pltpu.CompilerParams(vmem_limit_bytes=SMALL_VMEM_BYTES),
        cost_estimate=NO_COST,
        name="hand_on",
    )(value, *before)


def sum_kernel(last, plan_ref, place_ref, *refs):
    extra = 5 if last else 1
    count = len(refs) - extra - 5
    sources, band_ref = refs[:count], refs[count]
    window, spread, total, arrived = refs[-4:]
    step, steps = pl.program_id(0), pl.num_programs(0)
    slots, points, rows, length = window.shape
    panels = (plan_ref.shape[0] - 2) // 3
    entries = panels * (2 if last else 1)
    wanted = plan_ref[3 * panels + (1 if last else 0)]
    half = spread.shape[1] // points
    width = 2 * half

    @pl.when(step == 0)
    def _():
        for slot in range(slots):
            chosen = jnp.clip(plan_ref[plan_ref[entries + slot]] - (FIRST_SOURCES if last else 0), 0, count - 1)
            for index, source in enumerate(sources):
                @pl.when((slot < wanted) & (chosen == index))
                def _():
                    pltpu.make_async_copy(source, window.at[slot], arrived.at[slot]).start()

    low = lax.broadcasted_iota(jnp.int32, (rows, width), 1) < half

    @pl.when(step < wanted)
    def _():
        pltpu.make_async_copy(sources[0], window.at[step], arrived.at[step]).wait()
        for j in range(points // 2):
            for c in range(length // width):
                first = window[step, 2 * j, :, c * width : (c + 1) * width].astype(jnp.float32)
                second = window[step, 2 * j + 1, :, c * width : (c + 1) * width].astype(jnp.float32)
                even = jnp.where(low, first, pltpu.roll(second, half, 1))
                odd = jnp.where(low, pltpu.roll(first, half, 1), second)
                spread[2 * c * rows : (2 * c + 1) * rows, j * width : (j + 1) * width] = even.astype(jnp.bfloat16)
                spread[(2 * c + 1) * rows : (2 * c + 2) * rows, j * width : (j + 1) * width] = odd.astype(jnp.bfloat16)
        product = jnp.dot(spread[...], band_ref[...], preferred_element_type=jnp.float32)

        @pl.when(step == 0)
        def _():
            total[...] = product

        @pl.when(step > 0)
        def _():
            total[...] += product

    @pl.when((step == 0) & (wanted == 0))
    def _():
        total[...] = jnp.zeros_like(total)

    @pl.when(step == steps - 1)
    def _():
        for s in range(total.shape[1] // width):

            def part(b):
                return total[b * rows : (b + 1) * rows, s * width : (s + 1) * width]

            for c in range(length // width):
                before = part(2 * c - 1) if c > 0 else jnp.zeros((rows, width), jnp.float32)
                summed = part(2 * c) + pltpu.roll(jnp.where(low, part(2 * c + 1), before), half, 1)
                span = slice(c * width, (c + 1) * width)
                if last:
                    early_ref, mine_ref, other_ref, out_mine_ref, out_other_ref = refs[count + 1 : -4]
                    shots = mine_ref.shape[0]
                    data_ref, out_ref = (mine_ref, out_mine_ref) if s < shots else (other_ref, out_other_ref)
                    summed = summed + early_ref[s, :, span]
                    here = data_ref[s % shots, :, span].astype(jnp.float32)
                    out_ref[s % shots, :, span] = (here - summed).astype(jnp.bfloat16)
                else:
                    refs[count + 1][s, :, span] = summed


def sum_of(plan, place, sources, bands, steps, taps, late=None):
    points, rows, length = sources[0].shape
    panels = (plan.shape[0] - 2) // 3
    height, columns = bands.shape[0] // panels, bands.shape[1]
    shots = columns // (2 * taps)
    last = late is not None
    entries = panels * (2 if last else 1)

    def band_place(step, plan, place):
        wanted = plan[3 * panels + (1 if last else 0)]
        return (plan[entries + jnp.maximum(jnp.minimum(step, wanted - 1), 0)], 0)

    in_specs = [ANYWHERE] * len(sources) + [pl.BlockSpec((height, columns), band_place)]
    operands = [*sources, bands]
    if last:
        chunk, early, data, other_data = late
        half = shots // 2
        piece = jax.ShapeDtypeStruct((half, rows, length), jnp.bfloat16)
        in_specs += [
            pl.BlockSpec((shots, rows, length), lambda step, plan, place: (0, 0, 0)),
            pl.BlockSpec((half, rows, length), lambda step, plan, place: (0, place[1] * CHUNKS + chunk, 0)),
            pl.BlockSpec((half, rows, length), lambda step, plan, place: (0, chunk, 0)),
        ]
        operands += [early, data, other_data]
        out_shape = (piece, piece)
        out_specs = [pl.BlockSpec((half, rows, length), lambda step, plan, place: (0, 0, 0))] * 2
    else:
        out_shape = jax.ShapeDtypeStruct((shots, rows, length), jnp.float32)
        out_specs = pl.BlockSpec((shots, rows, length), lambda step, plan, place: (0, 0, 0))
    tall = rows * length // taps
    return pl.pallas_call(
        functools.partial(sum_kernel, last),
        out_shape=out_shape,
        grid_spec=pltpu.PrefetchScalarGridSpec(
            num_scalar_prefetch=2,
            grid=(steps,),
            in_specs=in_specs,
            out_specs=out_specs,
            scratch_shapes=[
                pltpu.VMEM((steps, points, rows, length), jnp.bfloat16),
                pltpu.VMEM((tall, height), jnp.bfloat16),
                pltpu.VMEM((tall, columns), jnp.float32),
                pltpu.SemaphoreType.DMA((steps,)),
            ],
        ),
        compiler_params=pltpu.CompilerParams(vmem_limit_bytes=VMEM_BYTES),
        cost_estimate=pl.CostEstimate(flops=2 * tall * steps * height * columns, bytes_accessed=2 * steps * height * columns, transcendentals=0),
        name="residual" if last else "early_sum",
    )(plan, place, *operands)


def assemble_kernel(place_ref, *refs):
    pieces, out_ref, sems = refs[:-2], refs[-2], refs[-1]
    rows = pieces[0].shape[1]
    copies = []
    for index, piece in enumerate(pieces):
        side = place_ref[1] if index < CHUNKS else 1 - place_ref[1]
        start = pl.multiple_of((side * CHUNKS + index % CHUNKS) * rows, rows)
        copies.append(pltpu.make_async_copy(piece, out_ref.at[:, pl.ds(start, rows), :], sems.at[index]))
    for copy in copies:
        copy.start()
    for copy in copies:
        copy.wait()


def assemble(place, pieces, like):
    return pl.pallas_call(
        assemble_kernel,
        out_shape=jax.ShapeDtypeStruct(like.shape, like.dtype),
        in_specs=[IN_SMEM] + [pl.BlockSpec(memory_space=pl.ANY)] * len(pieces),
        out_specs=ANYWHERE,
        scratch_shapes=[pltpu.SemaphoreType.DMA((len(pieces),))],
        compiler_params=pltpu.CompilerParams(vmem_limit_bytes=SMALL_VMEM_BYTES),
        cost_estimate=NO_COST,
        name="assemble",
    )(place, *pieces)


def any_of(flags):
    return functools.reduce(jnp.logical_or, flags)


def exchange(data, surface_traces, primaries, panel_owner, place, third):
    panels = panel_owner.shape[0]
    side = data.shape[1] // 2
    rows = side // CHUNKS
    taps = primaries.shape[2]
    core = lax.rem(lax.axis_index("shot"), 2)
    plan, full = plan_of(panel_owner, place, data.shape[2])
    ring = lax.axis_size("rcv")
    there = jnp.concatenate([lax.dynamic_slice_in_dim(array, (1 - core) * side, side, axis=1) for array in (surface_traces, data)])
    met = flip(there, CORE)
    other_data = met[surface_traces.shape[0] :]
    ahead = lax.ppermute(primaries, "rcv", [(i, i ^ 1) for i in range(ring)])
    blocks, bit = jnp.stack([primaries, ahead]), 2
    blocks = jnp.concatenate([blocks, flip(blocks, CORE)], axis=1)
    own_a, own_b = [], []
    for chunk in range(CHUNKS):
        a, b = pick(chunk, panel_owner, place, surface_traces, met, [ahead] + own_a if own_a else [plan])
        own_a.append(a)
        own_b.append(b)
    across, down = [flip(a, ACROSS) for a in own_a], [flip(b, DOWN) for b in own_b]
    blocks = hand_on(blocks, [across[0], down[0]])
    while bit < ring:
        blocks = jnp.concatenate([blocks, lax.ppermute(blocks, "rcv", [(i, i ^ bit) for i in range(ring)])])
        bit *= 2
    blocks = jnp.pad(blocks.astype(jnp.float32), ((0, 0), (0, 0), (0, 0), (0, taps)))
    bands, full_later = bands_of(blocks, place, full)
    rows_full = [full] + [full_later] * (CHUNKS - 1)
    for_across = [jnp.where(row[0] > 0, own, met) for row, own, met in zip(rows_full, own_b, down)]
    for_down = [jnp.where(row[0] > 0, own, met) for row, own, met in zip(rows_full, own_a, across)]

    kept, returned = [], []
    for chunk in range(CHUNKS):
        first = [own_a[chunk], own_b[chunk], across[chunk], down[chunk]]
        second = [flip(for_across[chunk], ACROSS), flip(for_down[chunk], DOWN)]
        if third:
            second += [flip(second[1], ACROSS), flip(second[0], DOWN)]
        early = sum_of(plan, place, first, bands, panels, taps)
        mine, others = sum_of(plan, place, second, bands, panels - 1 if third else 2, taps, (chunk, early, data, other_data))
        kept.append(mine)
        returned.append(flip(others, CORE))
    return assemble(place, kept + returned, data)


def square_shards(data, surface_traces, primaries, panel_owner):
    me = lax.axis_index("shot")
    place = jnp.stack([me // 2, me % 2, lax.axis_index("rcv")]).astype(jnp.int32)
    holds_two = [jnp.sum(panel_owner // 2 == other) == 2 for other in range(SQUARE // 2)]
    neighbours_full = any_of([holds_two[at] & holds_two[at ^ bit] for at in range(SQUARE // 2) for bit in (1, 2) if at < at ^ bit])
    arguments = (data, surface_traces, primaries, panel_owner, place)
    residual = exchange(*arguments, False)
    return lax.while_loop(lambda state: state[0], lambda state: (jnp.bool_(False), exchange(*arguments, True)), (neighbours_full, residual))[1]


def solution(mesh):
    placed = (P("shot", "rcv", None), P("shot", "rcv", None), P("shot", "rcv", None), P())
    shards = square_shards if mesh.shape["shot"] == SQUARE else summed_broadcasts
    return jax.shard_map(shards, mesh=mesh, in_specs=placed, out_specs=P("shot", "rcv", None), check_vma=False)
```

```python
import functools

import jax
import jax.numpy as jnp
from jax import lax
from jax.experimental import pallas as pl
from jax.experimental.pallas import tpu as pltpu
from jax.sharding import PartitionSpec as P

CORE, ACROSS, DOWN = 1, 2, 4
SQUARE = 8
CHUNKS = 2
FIRST_SOURCES = 4
VMEM_BYTES = 16 * 1024 * 1024
SMALL_VMEM_BYTES = 2 * 1024 * 1024
IN_SMEM = pl.BlockSpec(memory_space=pltpu.SMEM)
ANYWHERE = pl.BlockSpec(memory_space=pl.ANY)
NO_COST = pl.CostEstimate(flops=0, bytes_accessed=0, transcendentals=0)


def broadcast(value, axis, root):
    mine = lax.axis_index(axis) == root
    return lax.psum(jnp.where(mine, value, jnp.zeros_like(value)), axis)


def shift_table(taps, block):
    shape = (2, taps, block, block)
    lag_index, tap_index, in_index, out_index = (lax.broadcasted_iota(jnp.int32, shape, dim) for dim in range(4))
    distance = out_index - in_index + lag_index * block
    return (distance == tap_index).astype(jnp.bfloat16)


def band_matrices(panel_prim, shift_ones):
    bands = jnp.einsum("skt,ltio->lskio", panel_prim, shift_ones, preferred_element_type=jnp.float32)
    return bands.astype(jnp.bfloat16)


def convolve(traces, bands, block):
    point_count, row_count, length = traces.shape
    blocks = traces.reshape(point_count, row_count, length // block, block)
    earlier = jnp.concatenate([jnp.zeros_like(blocks[:, :, :1]), blocks[:, :, :-1]], axis=2)
    stacked = jnp.stack([blocks, earlier])
    product = jnp.einsum("lkrbi,lskio->srbo", stacked, bands, preferred_element_type=jnp.float32)
    return product.reshape(bands.shape[1], row_count, length)


def summed_broadcasts(data, surface_traces, primaries, panel_owner):
    points, taps = surface_traces.shape[0], primaries.shape[2]
    shift_ones = shift_table(taps, 2 * taps)
    summed = jnp.zeros(data.shape, jnp.float32)
    panels_here = primaries.shape[1] // points
    for panel_id in range(panel_owner.shape[0]):
        first_point = panel_id % panels_here * points
        panel_prim = broadcast(primaries, "rcv", panel_id // panels_here)[:, first_point : first_point + points]
        traces = broadcast(surface_traces, "shot", panel_owner[panel_id])
        summed = summed + convolve(traces, band_matrices(panel_prim, shift_ones), 2 * taps)
    return (data.astype(jnp.float32) - summed).astype(jnp.bfloat16)


def flip(value, bit):
    return lax.ppermute(value, "shot", [(i, i ^ bit) for i in range(SQUARE)])


def band_kernel(place_ref, taps_ref, full_ref, band_ref, full_out_ref):
    shots, points, width = taps_ref.shape[1:]
    rows = width // 2

    def point(k, carry):
        for s in range(shots):
            row = taps_ref[0, s, pl.ds(k, 1), :]
            spread = pltpu.roll(jnp.broadcast_to(row, (rows, width)), 0, 1, stride=1, stride_axis=0)
            band_ref[pl.ds(pl.multiple_of(k * rows, rows), rows), s * width : (s + 1) * width] = spread.astype(jnp.bfloat16)
        return carry

    lax.fori_loop(0, points, point, 0)
    full_out_ref[...] = full_ref[...]


def bands_of(blocks, place, full):
    panels, shots, points, width = blocks.shape
    height = points * width // 2
    row = pl.BlockSpec(full.shape, lambda p, place: (0, 0))
    return pl.pallas_call(
        band_kernel,
        out_shape=(jax.ShapeDtypeStruct((panels * height, shots * width), jnp.bfloat16), jax.ShapeDtypeStruct(full.shape, full.dtype)),
        grid_spec=pltpu.PrefetchScalarGridSpec(
            num_scalar_prefetch=1,
            grid=(panels,),
            in_specs=[pl.BlockSpec((1, shots, points, width), lambda p, place: (place[2] ^ p, 0, 0, 0)), row],
            out_specs=[pl.BlockSpec((height, shots * width), lambda p, place: (p, 0)), row],
        ),
        compiler_params=pltpu.CompilerParams(vmem_limit_bytes=VMEM_BYTES),
        cost_estimate=pl.CostEstimate(flops=panels * height * shots * width * 8, bytes_accessed=panels * height * shots * width * 2, transcendentals=0),
        name="bands",
    )(place, blocks, full)


def source_of(panel, owner_ref, chip):
    panels = owner_ref.shape[0]

    def held(place):
        count = jnp.int32(0)
        for other in range(panels):
            count = count + (owner_ref[other] // 2 == place).astype(jnp.int32)
        return count

    owner = owner_ref[panel]
    there, second = owner // 2, lax.rem(owner, 2) == 1
    both = held(there) == 2
    across_full, down_full = held(chip ^ 1) == 2, held(chip ^ 2) == 2
    own = jnp.where(both & second, 1, 0)
    across = jnp.where(both & second, 4, 2)
    down = jnp.where(both & jnp.logical_not(second), 5, 3)
    single = jnp.where(down_full, 4, 5)
    double = jnp.where(second, jnp.where(across_full, 7, 4), jnp.where(down_full, 6, 5))
    diagonal = jnp.where(both, double, single)
    return jnp.where(there == chip, own, jnp.where(there == (chip ^ 1), across, jnp.where(there == (chip ^ 2), down, diagonal)))


def write_plan(owner_ref, place_ref, plan_ref):
    panels = owner_ref.shape[0]
    early, late = jnp.int32(0), jnp.int32(0)
    for entry in range(3 * panels):
        plan_ref[entry] = jnp.int32(0)
    for panel in range(panels):
        source = source_of(panel, owner_ref, place_ref[0])
        plan_ref[panel] = source
        plan_ref[panels + early] = jnp.int32(panel)
        plan_ref[2 * panels + late] = jnp.int32(panel)
        met_first = source < FIRST_SOURCES
        early = early + jnp.where(met_first, 1, 0)
        late = late + jnp.where(met_first, 0, 1)
    plan_ref[3 * panels] = early
    plan_ref[3 * panels + 1] = late


def pick_kernel(chunk, owner_ref, place_ref, slot_ref, met_ref, *refs):
    chip, core = place_ref[0], place_ref[1]
    first_owns, second_owns = jnp.bool_(False), jnp.bool_(False)
    for panel in range(owner_ref.shape[0]):
        first_owns = first_owns | (owner_ref[panel] == 2 * chip)
        second_owns = second_owns | (owner_ref[panel] == 2 * chip + 1)
    *others, a_ref, b_ref, sems = refs
    outs = (a_ref, b_ref)
    points, rows, _ = a_ref.shape
    here_ref = slot_ref.at[:, pl.ds(pl.multiple_of((core * CHUNKS + chunk) * rows, rows), rows), :]
    there_ref = met_ref.at[:, pl.ds(chunk * rows, rows), :]
    for index, mine in enumerate((first_owns == (core == 0), second_owns == (core == 1))):
        @pl.when(mine)
        def _():
            pltpu.make_async_copy(here_ref, outs[index], sems.at[index]).start()

        @pl.when(jnp.logical_not(mine))
        def _():
            pltpu.make_async_copy(there_ref, outs[index], sems.at[index]).start()

    if chunk == 1:
        plan_ref, full_ref = others[-2:]
        write_plan(owner_ref, place_ref, plan_ref)
        full_ref[...] = jnp.full(full_ref.shape, jnp.where(first_owns & second_owns, 1.0, 0.0), jnp.float32)
    for index in range(2):
        pltpu.make_async_copy(there_ref, outs[index], sems.at[index]).wait()


def pick(chunk, owner, place, slot, met, before):
    points, length = slot.shape[0], slot.shape[2]
    in_vmem = pl.BlockSpec(memory_space=pltpu.VMEM)
    outs = [jax.ShapeDtypeStruct((points, met.shape[1] // CHUNKS, length), slot.dtype)] * 2
    specs = [in_vmem] * 2
    if chunk == 1:
        outs = [jax.ShapeDtypeStruct((3 * owner.shape[0] + 2,), jnp.int32), jax.ShapeDtypeStruct((1, length), jnp.float32)] + outs
        specs = [IN_SMEM, in_vmem] + specs
    return pl.pallas_call(
        functools.partial(pick_kernel, chunk),
        out_shape=tuple(outs),
        in_specs=[IN_SMEM] * 2 + [ANYWHERE] * (2 + len(before)),
        out_specs=specs,
        scratch_shapes=[pltpu.SemaphoreType.DMA((2,))],
        compiler_params=pltpu.CompilerParams(vmem_limit_bytes=2 * SMALL_VMEM_BYTES),
        cost_estimate=NO_COST,
        name="pick",
    )(owner, place, slot, met, *before)


def cut_kernel(place_ref, array_ref, *refs):
    refs[-1][...] = array_ref[...]


def cut(array, place, before):
    block = (array.shape[0], array.shape[1] // 2, array.shape[2])
    return pl.pallas_call(
        cut_kernel,
        out_shape=jax.ShapeDtypeStruct(block, array.dtype),
        grid_spec=pltpu.PrefetchScalarGridSpec(
            num_scalar_prefetch=1,
            grid=(1,),
            in_specs=[pl.BlockSpec(block, lambda step, place: (0, 1 - place[1], 0))] + [ANYWHERE] * len(before),
            out_specs=pl.BlockSpec(block, lambda step, place: (0, 0, 0)),
        ),
        compiler_params=pltpu.CompilerParams(vmem_limit_bytes=2 * SMALL_VMEM_BYTES),
        cost_estimate=NO_COST,
        name="cut",
    )(place, array, *before)


def hand_on_kernel(value_ref, *refs):
    refs[-1][...] = value_ref[...]


def hand_on(value, before):
    whole = pl.BlockSpec(memory_space=pltpu.VMEM)
    return pl.pallas_call(
        hand_on_kernel,
        out_shape=jax.ShapeDtypeStruct(value.shape, value.dtype),
        in_specs=[whole] + [ANYWHERE] * len(before),
        out_specs=whole,
        compiler_params=pltpu.CompilerParams(vmem_limit_bytes=SMALL_VMEM_BYTES),
        cost_estimate=NO_COST,
        name="hand_on",
    )(value, *before)


def sum_kernel(last, plan_ref, place_ref, *refs):
    extra = 5 if last else 1
    count = len(refs) - extra - 5
    sources, band_ref = refs[:count], refs[count]
    window, spread, total, arrived = refs[-4:]
    step, steps = pl.program_id(0), pl.num_programs(0)
    slots, points, rows, length = window.shape
    panels = (plan_ref.shape[0] - 2) // 3
    entries = panels * (2 if last else 1)
    wanted = plan_ref[3 * panels + (1 if last else 0)]
    half = spread.shape[1] // points
    width = 2 * half

    @pl.when(step == 0)
    def _():
        for slot in range(slots):
            chosen = jnp.clip(plan_ref[plan_ref[entries + slot]] - (FIRST_SOURCES if last else 0), 0, count - 1)
            for index, source in enumerate(sources):
                @pl.when((slot < wanted) & (chosen == index))
                def _():
                    pltpu.make_async_copy(source, window.at[slot], arrived.at[slot]).start()

    low = lax.broadcasted_iota(jnp.int32, (rows, width), 1) < half

    @pl.when(step < wanted)
    def _():
        pltpu.make_async_copy(sources[0], window.at[step], arrived.at[step]).wait()
        for j in range(points // 2):
            for c in range(length // width):
                first = window[step, 2 * j, :, c * width : (c + 1) * width].astype(jnp.float32)
                second = window[step, 2 * j + 1, :, c * width : (c + 1) * width].astype(jnp.float32)
                even = jnp.where(low, first, pltpu.roll(second, half, 1))
                odd = jnp.where(low, pltpu.roll(first, half, 1), second)
                spread[2 * c * rows : (2 * c + 1) * rows, j * width : (j + 1) * width] = even.astype(jnp.bfloat16)
                spread[(2 * c + 1) * rows : (2 * c + 2) * rows, j * width : (j + 1) * width] = odd.astype(jnp.bfloat16)
        product = jnp.dot(spread[...], band_ref[...], preferred_element_type=jnp.float32)

        @pl.when(step == 0)
        def _():
            total[...] = product

        @pl.when(step > 0)
        def _():
            total[...] += product

    @pl.when((step == 0) & (wanted == 0))
    def _():
        total[...] = jnp.zeros_like(total)

    @pl.when(step == steps - 1)
    def _():
        for s in range(total.shape[1] // width):

            def part(b):
                return total[b * rows : (b + 1) * rows, s * width : (s + 1) * width]

            for c in range(length // width):
                before = part(2 * c - 1) if c > 0 else jnp.zeros((rows, width), jnp.float32)
                summed = part(2 * c) + pltpu.roll(jnp.where(low, part(2 * c + 1), before), half, 1)
                span = slice(c * width, (c + 1) * width)
                if last:
                    early_ref, mine_ref, other_ref, out_mine_ref, out_other_ref = refs[count + 1 : -4]
                    shots = mine_ref.shape[0]
                    data_ref, out_ref = (mine_ref, out_mine_ref) if s < shots else (other_ref, out_other_ref)
                    summed = summed + early_ref[s, :, span]
                    here = data_ref[s % shots, :, span].astype(jnp.float32)
                    out_ref[s % shots, :, span] = (here - summed).astype(jnp.bfloat16)
                else:
                    refs[count + 1][s, :, span] = summed


def sum_of(plan, place, sources, bands, steps, taps, late=None):
    points, rows, length = sources[0].shape
    panels = (plan.shape[0] - 2) // 3
    height, columns = bands.shape[0] // panels, bands.shape[1]
    shots = columns // (2 * taps)
    last = late is not None
    entries = panels * (2 if last else 1)

    def band_place(step, plan, place):
        wanted = plan[3 * panels + (1 if last else 0)]
        return (plan[entries + jnp.maximum(jnp.minimum(step, wanted - 1), 0)], 0)

    in_specs = [ANYWHERE] * len(sources) + [pl.BlockSpec((height, columns), band_place)]
    operands = [*sources, bands]
    if last:
        chunk, early, data, other_data = late
        half = shots // 2
        piece = jax.ShapeDtypeStruct((half, rows, length), jnp.bfloat16)
        in_specs += [
            pl.BlockSpec((shots, rows, length), lambda step, plan, place: (0, 0, 0)),
            pl.BlockSpec((half, rows, length), lambda step, plan, place: (0, place[1] * CHUNKS + chunk, 0)),
            pl.BlockSpec((half, rows, length), lambda step, plan, place: (0, chunk, 0)),
        ]
        operands += [early, data, other_data]
        out_shape = (piece, piece)
        out_specs = [pl.BlockSpec((half, rows, length), lambda step, plan, place: (0, 0, 0))] * 2
    else:
        out_shape = jax.ShapeDtypeStruct((shots, rows, length), jnp.float32)
        out_specs = pl.BlockSpec((shots, rows, length), lambda step, plan, place: (0, 0, 0))
    tall = rows * length // taps
    return pl.pallas_call(
        functools.partial(sum_kernel, last),
        out_shape=out_shape,
        grid_spec=pltpu.PrefetchScalarGridSpec(
            num_scalar_prefetch=2,
            grid=(steps,),
            in_specs=in_specs,
            out_specs=out_specs,
            scratch_shapes=[
                pltpu.VMEM((steps, points, rows, length), jnp.bfloat16),
                pltpu.VMEM((tall, height), jnp.bfloat16),
                pltpu.VMEM((tall, columns), jnp.float32),
                pltpu.SemaphoreType.DMA((steps,)),
            ],
        ),
        compiler_params=pltpu.CompilerParams(vmem_limit_bytes=VMEM_BYTES),
        cost_estimate=pl.CostEstimate(flops=2 * tall * steps * height * columns, bytes_accessed=2 * steps * height * columns, transcendentals=0),
        name="residual" if last else "early_sum",
    )(plan, place, *operands)


def assemble_kernel(at, place_ref, *refs):
    pieces, out_ref, sems = refs[: len(at)], refs[-2], refs[-1]
    rows = pieces[0].shape[1]
    copies = []
    for index, piece in enumerate(pieces):
        swapped, chunk = at[index]
        side = 1 - place_ref[1] if swapped else place_ref[1]
        start = pl.multiple_of((side * CHUNKS + chunk) * rows, rows)
        copies.append(pltpu.make_async_copy(piece, out_ref.at[:, pl.ds(start, rows), :], sems.at[index]))
    for copy in copies:
        copy.start()
    for copy in copies:
        copy.wait()


def assemble(place, pieces, at, like, onto=None):
    given = () if onto is None else (onto,)
    return pl.pallas_call(
        functools.partial(assemble_kernel, at),
        out_shape=pltpu.HBM(like.shape, like.dtype),
        in_specs=[IN_SMEM] + [ANYWHERE] * (len(pieces) + len(given)),
        out_specs=ANYWHERE,
        scratch_shapes=[pltpu.SemaphoreType.DMA((len(pieces),))],
        input_output_aliases={1 + len(pieces): 0} if given else {},
        compiler_params=pltpu.CompilerParams(vmem_limit_bytes=SMALL_VMEM_BYTES),
        cost_estimate=NO_COST,
        name="assemble",
    )(place, *pieces, *given)


def any_of(flags):
    return functools.reduce(jnp.logical_or, flags)


def exchange(data, surface_traces, primaries, panel_owner, place, flag, third):
    panels = panel_owner.shape[0]
    side = data.shape[1] // 2
    rows = side // CHUNKS
    taps = primaries.shape[2]
    core = lax.rem(lax.axis_index("shot"), 2)
    ring = lax.axis_size("rcv")
    met = flip(lax.dynamic_slice_in_dim(surface_traces, (1 - core) * side, side, axis=1), CORE)
    ahead = lax.ppermute(primaries, "rcv", [(i, i ^ 1) for i in range(ring)])
    blocks, bit = jnp.stack([primaries, ahead]), 2
    blocks = jnp.concatenate([blocks, flip(blocks, CORE)], axis=1)
    own_a, own_b = [], []
    for chunk in range(CHUNKS):
        *extra, a, b = pick(chunk, panel_owner, place, surface_traces, met, [ahead, flag, own_a[-1]] if own_a else [])
        if extra:
            plan, full = extra
        own_a.append(a)
        own_b.append(b)
    other_data = flip(cut(data, place, [own_a[-1]]), CORE)
    across, down = [flip(a, ACROSS) for a in own_a], [flip(b, DOWN) for b in own_b]
    blocks = hand_on(blocks, [across[0], down[0], other_data])
    while bit < ring:
        blocks = jnp.concatenate([blocks, lax.ppermute(blocks, "rcv", [(i, i ^ bit) for i in range(ring)])])
        bit *= 2
    blocks = jnp.pad(blocks.astype(jnp.float32), ((0, 0), (0, 0), (0, 0), (0, taps)))
    bands, full_later = bands_of(blocks, place, full)
    rows_full = [full] + [full_later] * (CHUNKS - 1)
    for_across = [jnp.where(row[0] > 0, own, met) for row, own, met in zip(rows_full, own_b, down)]
    for_down = [jnp.where(row[0] > 0, own, met) for row, own, met in zip(rows_full, own_a, across)]

    kept, returned = [], []
    for chunk in range(CHUNKS):
        first = [own_a[chunk], own_b[chunk], across[chunk], down[chunk]]
        second = [flip(for_across[chunk], ACROSS), flip(for_down[chunk], DOWN)]
        if third:
            second += [flip(second[1], ACROSS), flip(second[0], DOWN)]
        early = sum_of(plan, place, first, bands, panels, taps)
        mine, others = sum_of(plan, place, second, bands, panels - 1 if third else 2, taps, (chunk, early, data, other_data))
        kept.append(mine)
        returned.append(flip(others, CORE))
    places = [(False, chunk) for chunk in range(CHUNKS)] + [(True, chunk) for chunk in range(CHUNKS)]
    residual = assemble(place, (kept + returned)[:-1], places[:-1], data)
    return assemble(place, returned[-1:], places[-1:], data, residual)


def square_shards(data, surface_traces, primaries, panel_owner):
    me = lax.axis_index("shot")
    place = jnp.stack([me // 2, me % 2, lax.axis_index("rcv")]).astype(jnp.int32)
    holds_two = [jnp.sum(panel_owner // 2 == other) == 2 for other in range(SQUARE // 2)]
    neighbours_full = any_of([holds_two[at] & holds_two[at ^ bit] for at in range(SQUARE // 2) for bit in (1, 2) if at < at ^ bit])
    arguments = (data, surface_traces, primaries, panel_owner, place, neighbours_full.astype(jnp.float32)[None])
    residual = exchange(*arguments, False)
    return lax.while_loop(lambda state: state[0], lambda state: (jnp.bool_(False), exchange(*arguments, True)), (neighbours_full, residual))[1]


def solution(mesh):
    placed = (P("shot", "rcv", None), P("shot", "rcv", None), P("shot", "rcv", None), P())
    shards = square_shards if mesh.shape["shot"] == SQUARE else summed_broadcasts
    return jax.shard_map(shards, mesh=mesh, in_specs=placed, out_specs=P("shot", "rcv", None), check_vma=False)
```

```python
import functools

import jax
import jax.numpy as jnp
from jax import lax
from jax.experimental import pallas as pl
from jax.experimental.pallas import tpu as pltpu
from jax.sharding import PartitionSpec as P

CORE, ACROSS, DOWN = 1, 2, 4
SQUARE = 8
CHUNKS = 2
FIRST_SOURCES = 4
VMEM_BYTES = 16 * 1024 * 1024
SMALL_VMEM_BYTES = 2 * 1024 * 1024
IN_SMEM = pl.BlockSpec(memory_space=pltpu.SMEM)
ANYWHERE = pl.BlockSpec(memory_space=pl.ANY)
NO_COST = pl.CostEstimate(flops=0, bytes_accessed=0, transcendentals=0)


def broadcast(value, axis, root):
    mine = lax.axis_index(axis) == root
    return lax.psum(jnp.where(mine, value, jnp.zeros_like(value)), axis)


def shift_table(taps, block):
    shape = (2, taps, block, block)
    lag_index, tap_index, in_index, out_index = (lax.broadcasted_iota(jnp.int32, shape, dim) for dim in range(4))
    distance = out_index - in_index + lag_index * block
    return (distance == tap_index).astype(jnp.bfloat16)


def band_matrices(panel_prim, shift_ones):
    bands = jnp.einsum("skt,ltio->lskio", panel_prim, shift_ones, preferred_element_type=jnp.float32)
    return bands.astype(jnp.bfloat16)


def convolve(traces, bands, block):
    point_count, row_count, length = traces.shape
    blocks = traces.reshape(point_count, row_count, length // block, block)
    earlier = jnp.concatenate([jnp.zeros_like(blocks[:, :, :1]), blocks[:, :, :-1]], axis=2)
    stacked = jnp.stack([blocks, earlier])
    product = jnp.einsum("lkrbi,lskio->srbo", stacked, bands, preferred_element_type=jnp.float32)
    return product.reshape(bands.shape[1], row_count, length)


def summed_broadcasts(data, surface_traces, primaries, panel_owner):
    points, taps = surface_traces.shape[0], primaries.shape[2]
    shift_ones = shift_table(taps, 2 * taps)
    summed = jnp.zeros(data.shape, jnp.float32)
    panels_here = primaries.shape[1] // points
    for panel_id in range(panel_owner.shape[0]):
        first_point = panel_id % panels_here * points
        panel_prim = broadcast(primaries, "rcv", panel_id // panels_here)[:, first_point : first_point + points]
        traces = broadcast(surface_traces, "shot", panel_owner[panel_id])
        summed = summed + convolve(traces, band_matrices(panel_prim, shift_ones), 2 * taps)
    return (data.astype(jnp.float32) - summed).astype(jnp.bfloat16)


def flip(value, bit):
    return lax.ppermute(value, "shot", [(i, i ^ bit) for i in range(SQUARE)])


def band_kernel(place_ref, taps_ref, full_ref, band_ref, full_out_ref):
    shots, points, width = taps_ref.shape[1:]
    rows = width // 2

    def point(k, carry):
        for s in range(shots):
            row = taps_ref[0, s, pl.ds(k, 1), :]
            spread = pltpu.roll(jnp.broadcast_to(row, (rows, width)), 0, 1, stride=1, stride_axis=0)
            band_ref[pl.ds(pl.multiple_of(k * rows, rows), rows), s * width : (s + 1) * width] = spread.astype(jnp.bfloat16)
        return carry

    lax.fori_loop(0, points, point, 0)
    full_out_ref[...] = full_ref[...]


def bands_of(blocks, place, full):
    panels, shots, points, width = blocks.shape
    height = points * width // 2
    row = pl.BlockSpec(full.shape, lambda p, place: (0, 0))
    return pl.pallas_call(
        band_kernel,
        out_shape=(jax.ShapeDtypeStruct((panels * height, shots * width), jnp.bfloat16), jax.ShapeDtypeStruct(full.shape, full.dtype)),
        grid_spec=pltpu.PrefetchScalarGridSpec(
            num_scalar_prefetch=1,
            grid=(panels,),
            in_specs=[pl.BlockSpec((1, shots, points, width), lambda p, place: (place[2] ^ p, 0, 0, 0)), row],
            out_specs=[pl.BlockSpec((height, shots * width), lambda p, place: (p, 0)), row],
        ),
        compiler_params=pltpu.CompilerParams(vmem_limit_bytes=VMEM_BYTES),
        cost_estimate=pl.CostEstimate(flops=panels * height * shots * width * 8, bytes_accessed=panels * height * shots * width * 2, transcendentals=0),
        name="bands",
    )(place, blocks, full)


def source_of(panel, owner_ref, chip):
    panels = owner_ref.shape[0]

    def held(place):
        count = jnp.int32(0)
        for other in range(panels):
            count = count + (owner_ref[other] // 2 == place).astype(jnp.int32)
        return count

    owner = owner_ref[panel]
    there, second = owner // 2, lax.rem(owner, 2) == 1
    both = held(there) == 2
    across_full, down_full = held(chip ^ 1) == 2, held(chip ^ 2) == 2
    own = jnp.where(both & second, 1, 0)
    across = jnp.where(both & second, 4, 2)
    down = jnp.where(both & jnp.logical_not(second), 5, 3)
    single = jnp.where(down_full, 4, 5)
    double = jnp.where(second, jnp.where(across_full, 7, 4), jnp.where(down_full, 6, 5))
    diagonal = jnp.where(both, double, single)
    return jnp.where(there == chip, own, jnp.where(there == (chip ^ 1), across, jnp.where(there == (chip ^ 2), down, diagonal)))


def write_plan(owner_ref, place_ref, plan_ref):
    panels = owner_ref.shape[0]
    early, late = jnp.int32(0), jnp.int32(0)
    for entry in range(3 * panels):
        plan_ref[entry] = jnp.int32(0)
    for panel in range(panels):
        source = source_of(panel, owner_ref, place_ref[0])
        plan_ref[panel] = source
        plan_ref[panels + early] = jnp.int32(panel)
        plan_ref[2 * panels + late] = jnp.int32(panel)
        met_first = source < FIRST_SOURCES
        early = early + jnp.where(met_first, 1, 0)
        late = late + jnp.where(met_first, 0, 1)
    plan_ref[3 * panels] = early
    plan_ref[3 * panels + 1] = late
    held = [jnp.int32(0)] * (SQUARE // 2)
    for panel in range(panels):
        held = [count + (owner_ref[panel] // 2 == place).astype(jnp.int32) for place, count in enumerate(held)]
    full = [count == 2 for count in held]
    pairs = [full[place] & full[place ^ bit] for place in range(SQUARE // 2) for bit in (1, 2) if place < place ^ bit]
    plan_ref[3 * panels + 2] = functools.reduce(jnp.logical_or, pairs).astype(jnp.int32)


def pick_kernel(chunk, owner_ref, place_ref, here_ref, there_ref, *refs):
    chip, core = place_ref[0], place_ref[1]
    first_owns, second_owns = jnp.bool_(False), jnp.bool_(False)
    for panel in range(owner_ref.shape[0]):
        first_owns = first_owns | (owner_ref[panel] == 2 * chip)
        second_owns = second_owns | (owner_ref[panel] == 2 * chip + 1)
    *others, a_ref, b_ref, sems = refs
    outs = (a_ref, b_ref)
    for index, mine in enumerate((first_owns == (core == 0), second_owns == (core == 1))):
        @pl.when(mine)
        def _():
            pltpu.make_async_copy(here_ref, outs[index], sems.at[index]).start()

        @pl.when(jnp.logical_not(mine))
        def _():
            pltpu.make_async_copy(there_ref, outs[index], sems.at[index]).start()

    if chunk == 1:
        plan_ref, full_ref = others[-2:]
        write_plan(owner_ref, place_ref, plan_ref)
        full_ref[...] = jnp.full(full_ref.shape, jnp.where(first_owns & second_owns, 1.0, 0.0), jnp.float32)
    for index in range(2):
        pltpu.make_async_copy(there_ref, outs[index], sems.at[index]).wait()


def pick(chunk, owner, place, here, there, before):
    length = here.shape[2]
    in_vmem = pl.BlockSpec(memory_space=pltpu.VMEM)
    outs = [jax.ShapeDtypeStruct(here.shape, here.dtype)] * 2
    specs = [in_vmem] * 2
    if chunk == 1:
        outs = [jax.ShapeDtypeStruct((3 * owner.shape[0] + 3,), jnp.int32), jax.ShapeDtypeStruct((1, length), jnp.float32)] + outs
        specs = [IN_SMEM, in_vmem] + specs
    return pl.pallas_call(
        functools.partial(pick_kernel, chunk),
        out_shape=tuple(outs),
        in_specs=[IN_SMEM] * 2 + [ANYWHERE] * (2 + len(before)),
        out_specs=specs,
        scratch_shapes=[pltpu.SemaphoreType.DMA((2,))],
        compiler_params=pltpu.CompilerParams(vmem_limit_bytes=2 * SMALL_VMEM_BYTES),
        cost_estimate=NO_COST,
        name="pick",
    )(owner, place, here, there, *before)


def cut_kernel(place_ref, array_ref, *refs):
    refs[-1][...] = array_ref[...]


def cut(array, place, before):
    block = (array.shape[0], array.shape[1] // 2, array.shape[2])
    return pl.pallas_call(
        cut_kernel,
        out_shape=jax.ShapeDtypeStruct(block, array.dtype),
        grid_spec=pltpu.PrefetchScalarGridSpec(
            num_scalar_prefetch=1,
            grid=(1,),
            in_specs=[pl.BlockSpec(block, lambda step, place: (0, 1 - place[1], 0))] + [ANYWHERE] * len(before),
            out_specs=pl.BlockSpec(block, lambda step, place: (0, 0, 0)),
        ),
        compiler_params=pltpu.CompilerParams(vmem_limit_bytes=2 * SMALL_VMEM_BYTES),
        cost_estimate=NO_COST,
        name="cut",
    )(place, array, *before)


def hand_on_kernel(value_ref, *refs):
    refs[-1][...] = value_ref[...]


def hand_on(value, before):
    whole = pl.BlockSpec(memory_space=pltpu.VMEM)
    return pl.pallas_call(
        hand_on_kernel,
        out_shape=jax.ShapeDtypeStruct(value.shape, value.dtype),
        in_specs=[whole] + [ANYWHERE] * len(before),
        out_specs=whole,
        compiler_params=pltpu.CompilerParams(vmem_limit_bytes=SMALL_VMEM_BYTES),
        cost_estimate=NO_COST,
        name="hand_on",
    )(value, *before)


def sum_kernel(last, plan_ref, place_ref, *refs):
    extra = 5 if last else 1
    count = len(refs) - extra - 5
    sources, band_ref = refs[:count], refs[count]
    window, spread, total, arrived = refs[-4:]
    step, steps = pl.program_id(0), pl.num_programs(0)
    slots, points, rows, length = window.shape
    panels = plan_ref.shape[0] // 3 - 1
    entries = panels * (2 if last else 1)
    wanted = plan_ref[3 * panels + (1 if last else 0)]
    half = spread.shape[1] // points
    width = 2 * half

    @pl.when(step == 0)
    def _():
        for slot in range(slots):
            chosen = jnp.clip(plan_ref[plan_ref[entries + slot]] - (FIRST_SOURCES if last else 0), 0, count - 1)
            for index, source in enumerate(sources):
                @pl.when((slot < wanted) & (chosen == index))
                def _():
                    pltpu.make_async_copy(source, window.at[slot], arrived.at[slot]).start()

    low = lax.broadcasted_iota(jnp.int32, (rows, width), 1) < half

    @pl.when(step < wanted)
    def _():
        pltpu.make_async_copy(sources[0], window.at[step], arrived.at[step]).wait()
        for j in range(points // 2):
            for c in range(length // width):
                first = window[step, 2 * j, :, c * width : (c + 1) * width].astype(jnp.float32)
                second = window[step, 2 * j + 1, :, c * width : (c + 1) * width].astype(jnp.float32)
                even = jnp.where(low, first, pltpu.roll(second, half, 1))
                odd = jnp.where(low, pltpu.roll(first, half, 1), second)
                spread[2 * c * rows : (2 * c + 1) * rows, j * width : (j + 1) * width] = even.astype(jnp.bfloat16)
                spread[(2 * c + 1) * rows : (2 * c + 2) * rows, j * width : (j + 1) * width] = odd.astype(jnp.bfloat16)
        product = jnp.dot(spread[...], band_ref[...], preferred_element_type=jnp.float32)

        @pl.when(step == 0)
        def _():
            total[...] = product

        @pl.when(step > 0)
        def _():
            total[...] += product

    @pl.when((step == 0) & (wanted == 0))
    def _():
        total[...] = jnp.zeros_like(total)

    @pl.when(step == steps - 1)
    def _():
        for s in range(total.shape[1] // width):

            def part(b):
                return total[b * rows : (b + 1) * rows, s * width : (s + 1) * width]

            for c in range(length // width):
                before = part(2 * c - 1) if c > 0 else jnp.zeros((rows, width), jnp.float32)
                summed = part(2 * c) + pltpu.roll(jnp.where(low, part(2 * c + 1), before), half, 1)
                span = slice(c * width, (c + 1) * width)
                if last:
                    early_ref, mine_ref, other_ref, out_mine_ref, out_other_ref = refs[count + 1 : -4]
                    shots = mine_ref.shape[0]
                    data_ref, out_ref = (mine_ref, out_mine_ref) if s < shots else (other_ref, out_other_ref)
                    summed = summed + early_ref[s, :, span]
                    here = data_ref[s % shots, :, span].astype(jnp.float32)
                    out_ref[s % shots, :, span] = (here - summed).astype(jnp.bfloat16)
                else:
                    refs[count + 1][s, :, span] = summed


def sum_of(plan, place, sources, bands, steps, taps, late=None):
    points, rows, length = sources[0].shape
    panels = plan.shape[0] // 3 - 1
    height, columns = bands.shape[0] // panels, bands.shape[1]
    shots = columns // (2 * taps)
    last = late is not None
    entries = panels * (2 if last else 1)

    def band_place(step, plan, place):
        wanted = plan[3 * panels + (1 if last else 0)]
        return (plan[entries + jnp.maximum(jnp.minimum(step, wanted - 1), 0)], 0)

    in_specs = [ANYWHERE] * len(sources) + [pl.BlockSpec((height, columns), band_place)]
    operands = [*sources, bands]
    if last:
        chunk, early, data, other_data = late
        half = shots // 2
        piece = jax.ShapeDtypeStruct((half, rows, length), jnp.bfloat16)
        in_specs += [
            pl.BlockSpec((shots, rows, length), lambda step, plan, place: (0, 0, 0)),
            pl.BlockSpec((half, rows, length), lambda step, plan, place: (0, place[1] * CHUNKS + chunk, 0)),
            pl.BlockSpec((half, rows, length), lambda step, plan, place: (0, chunk, 0)),
        ]
        operands += [early, data, other_data]
        out_shape = (piece, piece)
        out_specs = [pl.BlockSpec((half, rows, length), lambda step, plan, place: (0, 0, 0))] * 2
    else:
        out_shape = jax.ShapeDtypeStruct((shots, rows, length), jnp.float32)
        out_specs = pl.BlockSpec((shots, rows, length), lambda step, plan, place: (0, 0, 0))
    tall = rows * length // taps
    return pl.pallas_call(
        functools.partial(sum_kernel, last),
        out_shape=out_shape,
        grid_spec=pltpu.PrefetchScalarGridSpec(
            num_scalar_prefetch=2,
            grid=(steps,),
            in_specs=in_specs,
            out_specs=out_specs,
            scratch_shapes=[
                pltpu.VMEM((steps, points, rows, length), jnp.bfloat16),
                pltpu.VMEM((tall, height), jnp.bfloat16),
                pltpu.VMEM((tall, columns), jnp.float32),
                pltpu.SemaphoreType.DMA((steps,)),
            ],
        ),
        compiler_params=pltpu.CompilerParams(vmem_limit_bytes=VMEM_BYTES),
        cost_estimate=pl.CostEstimate(flops=2 * tall * steps * height * columns, bytes_accessed=2 * steps * height * columns, transcendentals=0),
        name="residual" if last else "early_sum",
    )(plan, place, *operands)


def assemble_kernel(at, place_ref, *refs):
    pieces, out_ref, sems = refs[: len(at)], refs[-2], refs[-1]
    rows = pieces[0].shape[1]
    copies = []
    for index, piece in enumerate(pieces):
        swapped, chunk = at[index]
        side = 1 - place_ref[1] if swapped else place_ref[1]
        start = pl.multiple_of((side * CHUNKS + chunk) * rows, rows)
        copies.append(pltpu.make_async_copy(piece, out_ref.at[:, pl.ds(start, rows), :], sems.at[index]))
    for copy in copies:
        copy.start()
    for copy in copies:
        copy.wait()


def assemble(place, pieces, at, like, onto=None):
    given = () if onto is None else (onto,)
    return pl.pallas_call(
        functools.partial(assemble_kernel, at),
        out_shape=pltpu.HBM(like.shape, like.dtype),
        in_specs=[IN_SMEM] + [ANYWHERE] * (len(pieces) + len(given)),
        out_specs=ANYWHERE,
        scratch_shapes=[pltpu.SemaphoreType.DMA((len(pieces),))],
        input_output_aliases={1 + len(pieces): 0} if given else {},
        compiler_params=pltpu.CompilerParams(vmem_limit_bytes=SMALL_VMEM_BYTES),
        cost_estimate=NO_COST,
        name="assemble",
    )(place, *pieces, *given)


def exchange(data, surface_traces, primaries, panel_owner, place, third):
    panels = panel_owner.shape[0]
    side = data.shape[1] // 2
    rows = side // CHUNKS
    taps = primaries.shape[2]
    core = lax.rem(lax.axis_index("shot"), 2)
    ring = lax.axis_size("rcv")
    ahead = lax.ppermute(primaries, "rcv", [(i, i ^ 1) for i in range(ring)])
    blocks, bit = jnp.stack([primaries, ahead]), 2
    blocks = jnp.concatenate([blocks, flip(blocks, CORE)], axis=1)
    own_a, own_b = [], []
    for chunk in range(CHUNKS):
        here, there = (lax.dynamic_slice_in_dim(surface_traces, at * side + chunk * rows, rows, axis=1) for at in (core, 1 - core))
        *extra, a, b = pick(chunk, panel_owner, place, here, flip(there, CORE), [ahead] if own_a else [])
        if extra:
            plan, full = extra
        own_a.append(a)
        own_b.append(b)
    across, down = [flip(a, ACROSS) for a in own_a], [flip(b, DOWN) for b in own_b]
    neighbours_full = plan[-1] > 0
    blocks = hand_on(blocks, [across[0], down[0], neighbours_full.astype(jnp.float32)[None]])
    while bit < ring:
        blocks = jnp.concatenate([blocks, lax.ppermute(blocks, "rcv", [(i, i ^ bit) for i in range(ring)])])
        bit *= 2
    blocks = jnp.pad(blocks.astype(jnp.float32), ((0, 0), (0, 0), (0, 0), (0, taps)))
    bands, full_later = bands_of(blocks, place, full)
    other_data = flip(cut(data, place, [full_later]), CORE)
    rows_full = [full] + [full_later] * (CHUNKS - 1)
    for_across = [jnp.where(row[0] > 0, own, met) for row, own, met in zip(rows_full, own_b, down)]
    for_down = [jnp.where(row[0] > 0, own, met) for row, own, met in zip(rows_full, own_a, across)]

    kept, returned = [], []
    for chunk in range(CHUNKS):
        first = [own_a[chunk], own_b[chunk], across[chunk], down[chunk]]
        second = [flip(for_across[chunk], ACROSS), flip(for_down[chunk], DOWN)]
        if third:
            second += [flip(second[1], ACROSS), flip(second[0], DOWN)]
        early = sum_of(plan, place, first, bands, panels, taps)
        mine, others = sum_of(plan, place, second, bands, panels - 1 if third else 2, taps, (chunk, early, data, other_data))
        kept.append(mine)
        returned.append(flip(others, CORE))
    places = [(False, chunk) for chunk in range(CHUNKS)] + [(True, chunk) for chunk in range(CHUNKS)]
    residual = assemble(place, (kept + returned)[:-1], places[:-1], data)
    return neighbours_full, assemble(place, returned[-1:], places[-1:], data, residual)


def square_shards(data, surface_traces, primaries, panel_owner):
    me = lax.axis_index("shot")
    place = jnp.stack([me // 2, me % 2, lax.axis_index("rcv")]).astype(jnp.int32)
    arguments = (data, surface_traces, primaries, panel_owner, place)
    again = lambda state: (jnp.bool_(False), exchange(*arguments, True)[1])
    return lax.while_loop(lambda state: state[0], again, exchange(*arguments, False))[1]


def solution(mesh):
    placed = (P("shot", "rcv", None), P("shot", "rcv", None), P("shot", "rcv", None), P())
    shards = square_shards if mesh.shape["shot"] == SQUARE else summed_broadcasts
    return jax.shard_map(shards, mesh=mesh, in_specs=placed, out_specs=P("shot", "rcv", None), check_vma=False)
```

```python
import functools

import jax
import jax.numpy as jnp
from jax import lax
from jax.experimental import pallas as pl
from jax.experimental.pallas import tpu as pltpu
from jax.sharding import PartitionSpec as P

CORE, ACROSS, DOWN = 1, 2, 4
SQUARE = 8
CHUNKS = 2
FIRST_SOURCES = 4
VMEM_BYTES = 16 * 1024 * 1024
SMALL_VMEM_BYTES = 2 * 1024 * 1024
IN_SMEM = pl.BlockSpec(memory_space=pltpu.SMEM)
ANYWHERE = pl.BlockSpec(memory_space=pl.ANY)
NO_COST = pl.CostEstimate(flops=0, bytes_accessed=0, transcendentals=0)


def broadcast(value, axis, root):
    mine = lax.axis_index(axis) == root
    return lax.psum(jnp.where(mine, value, jnp.zeros_like(value)), axis)


def shift_table(taps, block):
    shape = (2, taps, block, block)
    lag_index, tap_index, in_index, out_index = (lax.broadcasted_iota(jnp.int32, shape, dim) for dim in range(4))
    distance = out_index - in_index + lag_index * block
    return (distance == tap_index).astype(jnp.bfloat16)


def band_matrices(panel_prim, shift_ones):
    bands = jnp.einsum("skt,ltio->lskio", panel_prim, shift_ones, preferred_element_type=jnp.float32)
    return bands.astype(jnp.bfloat16)


def convolve(traces, bands, block):
    point_count, row_count, length = traces.shape
    blocks = traces.reshape(point_count, row_count, length // block, block)
    earlier = jnp.concatenate([jnp.zeros_like(blocks[:, :, :1]), blocks[:, :, :-1]], axis=2)
    stacked = jnp.stack([blocks, earlier])
    product = jnp.einsum("lkrbi,lskio->srbo", stacked, bands, preferred_element_type=jnp.float32)
    return product.reshape(bands.shape[1], row_count, length)


def summed_broadcasts(data, surface_traces, primaries, panel_owner):
    points, taps = surface_traces.shape[0], primaries.shape[2]
    shift_ones = shift_table(taps, 2 * taps)
    summed = jnp.zeros(data.shape, jnp.float32)
    panels_here = primaries.shape[1] // points
    for panel_id in range(panel_owner.shape[0]):
        first_point = panel_id % panels_here * points
        panel_prim = broadcast(primaries, "rcv", panel_id // panels_here)[:, first_point : first_point + points]
        traces = broadcast(surface_traces, "shot", panel_owner[panel_id])
        summed = summed + convolve(traces, band_matrices(panel_prim, shift_ones), 2 * taps)
    return (data.astype(jnp.float32) - summed).astype(jnp.bfloat16)


def flip(value, bit):
    return lax.ppermute(value, "shot", [(i, i ^ bit) for i in range(SQUARE)])


def band_kernel(place_ref, taps_ref, full_ref, band_ref, full_out_ref):
    shots, points, width = taps_ref.shape[1:]
    rows = width // 2

    def point(k, carry):
        for s in range(shots):
            row = taps_ref[0, s, pl.ds(k, 1), :]
            spread = pltpu.roll(jnp.broadcast_to(row, (rows, width)), 0, 1, stride=1, stride_axis=0)
            band_ref[pl.ds(pl.multiple_of(k * rows, rows), rows), s * width : (s + 1) * width] = spread.astype(jnp.bfloat16)
        return carry

    lax.fori_loop(0, points, point, 0)
    full_out_ref[...] = full_ref[...]


def bands_of(blocks, place, full):
    panels, shots, points, width = blocks.shape
    height = points * width // 2
    row = pl.BlockSpec(full.shape, lambda p, place: (0, 0))
    return pl.pallas_call(
        band_kernel,
        out_shape=(jax.ShapeDtypeStruct((panels * height, shots * width), jnp.bfloat16), jax.ShapeDtypeStruct(full.shape, full.dtype)),
        grid_spec=pltpu.PrefetchScalarGridSpec(
            num_scalar_prefetch=1,
            grid=(panels,),
            in_specs=[pl.BlockSpec((1, shots, points, width), lambda p, place: (place[2] ^ p, 0, 0, 0)), row],
            out_specs=[pl.BlockSpec((height, shots * width), lambda p, place: (p, 0)), row],
        ),
        compiler_params=pltpu.CompilerParams(vmem_limit_bytes=VMEM_BYTES),
        cost_estimate=pl.CostEstimate(flops=panels * height * shots * width * 8, bytes_accessed=panels * height * shots * width * 2, transcendentals=0),
        name="bands",
    )(place, blocks, full)


def source_of(panel, owner_ref, chip):
    panels = owner_ref.shape[0]

    def held(place):
        count = jnp.int32(0)
        for other in range(panels):
            count = count + (owner_ref[other] // 2 == place).astype(jnp.int32)
        return count

    owner = owner_ref[panel]
    there, second = owner // 2, lax.rem(owner, 2) == 1
    both = held(there) == 2
    across_full, down_full = held(chip ^ 1) == 2, held(chip ^ 2) == 2
    own = jnp.where(both & second, 1, 0)
    across = jnp.where(both & second, 4, 2)
    down = jnp.where(both & jnp.logical_not(second), 5, 3)
    single = jnp.where(down_full, 4, 5)
    double = jnp.where(second, jnp.where(across_full, 7, 4), jnp.where(down_full, 6, 5))
    diagonal = jnp.where(both, double, single)
    return jnp.where(there == chip, own, jnp.where(there == (chip ^ 1), across, jnp.where(there == (chip ^ 2), down, diagonal)))


def write_plan(owner_ref, place_ref, plan_ref):
    panels = owner_ref.shape[0]
    early, late = jnp.int32(0), jnp.int32(0)
    for entry in range(3 * panels):
        plan_ref[entry] = jnp.int32(0)
    for panel in range(panels):
        source = source_of(panel, owner_ref, place_ref[0])
        plan_ref[panel] = source
        plan_ref[panels + early] = jnp.int32(panel)
        plan_ref[2 * panels + late] = jnp.int32(panel)
        met_first = source < FIRST_SOURCES
        early = early + jnp.where(met_first, 1, 0)
        late = late + jnp.where(met_first, 0, 1)
    plan_ref[3 * panels] = early
    plan_ref[3 * panels + 1] = late
    held = [jnp.int32(0)] * (SQUARE // 2)
    for panel in range(panels):
        held = [count + (owner_ref[panel] // 2 == place).astype(jnp.int32) for place, count in enumerate(held)]
    full = [count == 2 for count in held]
    pairs = [full[place] & full[place ^ bit] for place in range(SQUARE // 2) for bit in (1, 2) if place < place ^ bit]
    plan_ref[3 * panels + 2] = functools.reduce(jnp.logical_or, pairs).astype(jnp.int32)


def pick_kernel(chunk, owner_ref, place_ref, here_ref, there_ref, *refs):
    chip, core = place_ref[0], place_ref[1]
    first_owns, second_owns = jnp.bool_(False), jnp.bool_(False)
    for panel in range(owner_ref.shape[0]):
        first_owns = first_owns | (owner_ref[panel] == 2 * chip)
        second_owns = second_owns | (owner_ref[panel] == 2 * chip + 1)
    *others, a_ref, b_ref, sems = refs
    outs = (a_ref, b_ref)
    for index, mine in enumerate((first_owns == (core == 0), second_owns == (core == 1))):
        @pl.when(mine)
        def _():
            pltpu.make_async_copy(here_ref, outs[index], sems.at[index]).start()

        @pl.when(jnp.logical_not(mine))
        def _():
            pltpu.make_async_copy(there_ref, outs[index], sems.at[index]).start()

    if chunk == 1:
        plan_ref, full_ref = others[-2:]
        write_plan(owner_ref, place_ref, plan_ref)
        full_ref[...] = jnp.full(full_ref.shape, jnp.where(first_owns & second_owns, 1.0, 0.0), jnp.float32)
    for index in range(2):
        pltpu.make_async_copy(there_ref, outs[index], sems.at[index]).wait()


def pick(chunk, owner, place, here, there, before):
    length = here.shape[2]
    in_vmem = pl.BlockSpec(memory_space=pltpu.VMEM)
    outs = [jax.ShapeDtypeStruct(here.shape, here.dtype)] * 2
    specs = [in_vmem] * 2
    if chunk == 1:
        outs = [jax.ShapeDtypeStruct((3 * owner.shape[0] + 3,), jnp.int32), jax.ShapeDtypeStruct((1, length), jnp.float32)] + outs
        specs = [IN_SMEM, in_vmem] + specs
    return pl.pallas_call(
        functools.partial(pick_kernel, chunk),
        out_shape=tuple(outs),
        in_specs=[IN_SMEM] * 2 + [ANYWHERE] * (2 + len(before)),
        out_specs=specs,
        scratch_shapes=[pltpu.SemaphoreType.DMA((2,))],
        compiler_params=pltpu.CompilerParams(vmem_limit_bytes=2 * SMALL_VMEM_BYTES),
        cost_estimate=NO_COST,
        name="pick",
    )(owner, place, here, there, *before)


def cut_kernel(place_ref, array_ref, *refs):
    refs[-1][...] = array_ref[...]


def cut(array, place, before):
    block = (array.shape[0], array.shape[1] // 2, array.shape[2])
    return pl.pallas_call(
        cut_kernel,
        out_shape=jax.ShapeDtypeStruct(block, array.dtype),
        grid_spec=pltpu.PrefetchScalarGridSpec(
            num_scalar_prefetch=1,
            grid=(1,),
            in_specs=[pl.BlockSpec(block, lambda step, place: (0, 1 - place[1], 0))] + [ANYWHERE] * len(before),
            out_specs=pl.BlockSpec(block, lambda step, place: (0, 0, 0)),
        ),
        compiler_params=pltpu.CompilerParams(vmem_limit_bytes=2 * SMALL_VMEM_BYTES),
        cost_estimate=NO_COST,
        name="cut",
    )(place, array, *before)


def hand_on_kernel(value_ref, *refs):
    refs[-1][...] = value_ref[...]


def hand_on(value, before):
    whole = pl.BlockSpec(memory_space=pltpu.VMEM)
    return pl.pallas_call(
        hand_on_kernel,
        out_shape=jax.ShapeDtypeStruct(value.shape, value.dtype),
        in_specs=[whole] + [ANYWHERE] * len(before),
        out_specs=whole,
        compiler_params=pltpu.CompilerParams(vmem_limit_bytes=SMALL_VMEM_BYTES),
        cost_estimate=NO_COST,
        name="hand_on",
    )(value, *before)


def sum_kernel(last, plan_ref, place_ref, *refs):
    extra = 5 if last else 1
    count = len(refs) - extra - 5
    sources, band_ref = refs[:count], refs[count]
    window, spread, total, arrived = refs[-4:]
    step, steps = pl.program_id(0), pl.num_programs(0)
    slots, points, rows, length = window.shape
    panels = plan_ref.shape[0] // 3 - 1
    entries = panels * (2 if last else 1)
    wanted = plan_ref[3 * panels + (1 if last else 0)]
    half = spread.shape[1] // points
    width = 2 * half

    @pl.when(step == 0)
    def _():
        for slot in range(slots):
            chosen = jnp.clip(plan_ref[plan_ref[entries + slot]] - (FIRST_SOURCES if last else 0), 0, count - 1)
            for index, source in enumerate(sources):
                @pl.when((slot < wanted) & (chosen == index))
                def _():
                    pltpu.make_async_copy(source, window.at[slot], arrived.at[slot]).start()

    low = lax.broadcasted_iota(jnp.int32, (rows, width), 1) < half

    @pl.when(step < wanted)
    def _():
        pltpu.make_async_copy(sources[0], window.at[step], arrived.at[step]).wait()
        for j in range(points // 2):
            for c in range(length // width):
                first = window[step, 2 * j, :, c * width : (c + 1) * width].astype(jnp.float32)
                second = window[step, 2 * j + 1, :, c * width : (c + 1) * width].astype(jnp.float32)
                even = jnp.where(low, first, pltpu.roll(second, half, 1))
                odd = jnp.where(low, pltpu.roll(first, half, 1), second)
                spread[2 * c * rows : (2 * c + 1) * rows, j * width : (j + 1) * width] = even.astype(jnp.bfloat16)
                spread[(2 * c + 1) * rows : (2 * c + 2) * rows, j * width : (j + 1) * width] = odd.astype(jnp.bfloat16)
        product = jnp.dot(spread[...], band_ref[...], preferred_element_type=jnp.float32)

        @pl.when(step == 0)
        def _():
            total[...] = product

        @pl.when(step > 0)
        def _():
            total[...] += product

    @pl.when((step == 0) & (wanted == 0))
    def _():
        total[...] = jnp.zeros_like(total)

    @pl.when(step == steps - 1)
    def _():
        for s in range(total.shape[1] // width):

            def part(b):
                return total[b * rows : (b + 1) * rows, s * width : (s + 1) * width]

            for c in range(length // width):
                before = part(2 * c - 1) if c > 0 else jnp.zeros((rows, width), jnp.float32)
                summed = part(2 * c) + pltpu.roll(jnp.where(low, part(2 * c + 1), before), half, 1)
                span = slice(c * width, (c + 1) * width)
                if last:
                    early_ref, mine_ref, other_ref, out_mine_ref, out_other_ref = refs[count + 1 : -4]
                    shots = mine_ref.shape[0]
                    data_ref, out_ref = (mine_ref, out_mine_ref) if s < shots else (other_ref, out_other_ref)
                    summed = summed + early_ref[s, :, span]
                    here = data_ref[s % shots, :, span].astype(jnp.float32)
                    out_ref[s % shots, :, span] = (here - summed).astype(jnp.bfloat16)
                else:
                    refs[count + 1][s, :, span] = summed


def sum_of(plan, place, sources, bands, steps, taps, late=None):
    points, rows, length = sources[0].shape
    panels = plan.shape[0] // 3 - 1
    height, columns = bands.shape[0] // panels, bands.shape[1]
    shots = columns // (2 * taps)
    last = late is not None
    entries = panels * (2 if last else 1)

    def band_place(step, plan, place):
        wanted = plan[3 * panels + (1 if last else 0)]
        return (plan[entries + jnp.maximum(jnp.minimum(step, wanted - 1), 0)], 0)

    in_specs = [ANYWHERE] * len(sources) + [pl.BlockSpec((height, columns), band_place)]
    operands = [*sources, bands]
    if last:
        chunk, early, data, other_data = late
        half = shots // 2
        piece = jax.ShapeDtypeStruct((half, rows, length), jnp.bfloat16)
        in_specs += [
            pl.BlockSpec((shots, rows, length), lambda step, plan, place: (0, 0, 0)),
            pl.BlockSpec((half, rows, length), lambda step, plan, place: (0, place[1] * CHUNKS + chunk, 0)),
            pl.BlockSpec((half, rows, length), lambda step, plan, place: (0, chunk, 0)),
        ]
        operands += [early, data, other_data]
        out_shape = (piece, piece)
        out_specs = [pl.BlockSpec((half, rows, length), lambda step, plan, place: (0, 0, 0))] * 2
    else:
        out_shape = jax.ShapeDtypeStruct((shots, rows, length), jnp.float32)
        out_specs = pl.BlockSpec((shots, rows, length), lambda step, plan, place: (0, 0, 0))
    tall = rows * length // taps
    return pl.pallas_call(
        functools.partial(sum_kernel, last),
        out_shape=out_shape,
        grid_spec=pltpu.PrefetchScalarGridSpec(
            num_scalar_prefetch=2,
            grid=(steps,),
            in_specs=in_specs,
            out_specs=out_specs,
            scratch_shapes=[
                pltpu.VMEM((steps, points, rows, length), jnp.bfloat16),
                pltpu.VMEM((tall, height), jnp.bfloat16),
                pltpu.VMEM((tall, columns), jnp.float32),
                pltpu.SemaphoreType.DMA((steps,)),
            ],
        ),
        compiler_params=pltpu.CompilerParams(vmem_limit_bytes=VMEM_BYTES),
        cost_estimate=pl.CostEstimate(flops=2 * tall * steps * height * columns, bytes_accessed=2 * steps * height * columns, transcendentals=0),
        name="residual" if last else "early_sum",
    )(plan, place, *operands)


def assemble_kernel(at, place_ref, *refs):
    pieces, out_ref, sems = refs[: len(at)], refs[-2], refs[-1]
    rows = pieces[0].shape[1]
    copies = []
    for index, piece in enumerate(pieces):
        swapped, chunk = at[index]
        side = 1 - place_ref[1] if swapped else place_ref[1]
        start = pl.multiple_of((side * CHUNKS + chunk) * rows, rows)
        copies.append(pltpu.make_async_copy(piece, out_ref.at[:, pl.ds(start, rows), :], sems.at[index]))
    for copy in copies:
        copy.start()
    for copy in copies:
        copy.wait()


def assemble(place, pieces, at, like, onto=None):
    given = () if onto is None else (onto,)
    return pl.pallas_call(
        functools.partial(assemble_kernel, at),
        out_shape=pltpu.HBM(like.shape, like.dtype),
        in_specs=[IN_SMEM] + [ANYWHERE] * (len(pieces) + len(given)),
        out_specs=ANYWHERE,
        scratch_shapes=[pltpu.SemaphoreType.DMA((len(pieces),))],
        input_output_aliases={1 + len(pieces): 0} if given else {},
        compiler_params=pltpu.CompilerParams(vmem_limit_bytes=SMALL_VMEM_BYTES),
        cost_estimate=NO_COST,
        name="assemble",
    )(place, *pieces, *given)


def exchange(data, surface_traces, primaries, panel_owner, place, third):
    panels = panel_owner.shape[0]
    side = data.shape[1] // 2
    rows = side // CHUNKS
    taps = primaries.shape[2]
    core = lax.rem(lax.axis_index("shot"), 2)
    ring = lax.axis_size("rcv")
    ahead = lax.ppermute(primaries, "rcv", [(i, i ^ 1) for i in range(ring)])
    blocks, bit = jnp.stack([primaries, ahead]), 2
    blocks = jnp.concatenate([blocks, flip(blocks, CORE)], axis=1)
    own_a, own_b = [], []
    for chunk in range(CHUNKS):
        here = lax.dynamic_slice_in_dim(surface_traces, core * side + chunk * rows, rows, axis=1)
        if chunk == 0:
            apart = surface_traces.reshape(surface_traces.shape[0], 2 * CHUNKS, rows, -1)
            there = lax.dynamic_index_in_dim(apart, (1 - core) * CHUNKS, axis=1, keepdims=False)
        else:
            there = lax.dynamic_slice_in_dim(surface_traces, (1 - core) * side + chunk * rows, rows, axis=1)
        *extra, a, b = pick(chunk, panel_owner, place, here, flip(there, CORE), [ahead] if own_a else [])
        if extra:
            plan, full = extra
        own_a.append(a)
        own_b.append(b)
    across, down = [flip(a, ACROSS) for a in own_a], [flip(b, DOWN) for b in own_b]
    neighbours_full = plan[-1] > 0
    blocks = hand_on(blocks, [across[0], down[0], neighbours_full.astype(jnp.float32)[None]])
    while bit < ring:
        blocks = jnp.concatenate([blocks, lax.ppermute(blocks, "rcv", [(i, i ^ bit) for i in range(ring)])])
        bit *= 2
    blocks = jnp.pad(blocks.astype(jnp.float32), ((0, 0), (0, 0), (0, 0), (0, taps)))
    bands, full_later = bands_of(blocks, place, full)
    other_data = flip(cut(data, place, [full_later]), CORE)
    rows_full = [full] + [full_later] * (CHUNKS - 1)
    for_across = [jnp.where(row[0] > 0, own, met) for row, own, met in zip(rows_full, own_b, down)]
    for_down = [jnp.where(row[0] > 0, own, met) for row, own, met in zip(rows_full, own_a, across)]

    kept, returned = [], []
    for chunk in range(CHUNKS):
        first = [own_a[chunk], own_b[chunk], across[chunk], down[chunk]]
        second = [flip(for_across[chunk], ACROSS), flip(for_down[chunk], DOWN)]
        if third:
            second += [flip(second[1], ACROSS), flip(second[0], DOWN)]
        early = sum_of(plan, place, first, bands, panels, taps)
        mine, others = sum_of(plan, place, second, bands, panels - 1 if third else 2, taps, (chunk, early, data, other_data))
        kept.append(mine)
        returned.append(flip(others, CORE))
    places = [(False, chunk) for chunk in range(CHUNKS)] + [(True, chunk) for chunk in range(CHUNKS)]
    residual = assemble(place, (kept + returned)[:-1], places[:-1], data)
    return neighbours_full, assemble(place, returned[-1:], places[-1:], data, residual)


def square_shards(data, surface_traces, primaries, panel_owner):
    me = lax.axis_index("shot")
    place = jnp.stack([me // 2, me % 2, lax.axis_index("rcv")]).astype(jnp.int32)
    arguments = (data, surface_traces, primaries, panel_owner, place)
    again = lambda state: (jnp.bool_(False), exchange(*arguments, True)[1])
    return lax.while_loop(lambda state: state[0], again, exchange(*arguments, False))[1]


def solution(mesh):
    placed = (P("shot", "rcv", None), P("shot", "rcv", None), P("shot", "rcv", None), P())
    shards = square_shards if mesh.shape["shot"] == SQUARE else summed_broadcasts
    return jax.shard_map(shards, mesh=mesh, in_specs=placed, out_specs=P("shot", "rcv", None), check_vma=False)
```
